32 devices in a mesh: lat: 8 (over z, y), lon: 4 (over x, core).
Axes of the slice: x: 2, y: 2, z: 4, core: 2. Of those that a mesh axis runs over, the one named last changes fastest.
Arguments:
- tokens: bfloat16 [24, 256, 512], P('lat', 'lon'), may hold values from -6 to 6
- ocean_count: int32 [24, 4], P('lat', 'lon'), may hold values from 1 to 64
- w_qkv: bfloat16 [512, 1536], replicated, may hold values from -0.25 to 0.25
- w_out: bfloat16 [512, 512], replicated, may hold values from -0.25 to 0.25
- w_up: bfloat16 [512, 1024], replicated, may hold values from -0.25 to 0.25
- w_down: bfloat16 [1024, 512], replicated, may hold values from -0.1875 to 0.1875
- cotangent: bfloat16 [24, 256, 512], P('lat', 'lon'), may hold values from -6 to 6
Outputs:
- block_out: bfloat16 [24, 256, 512], P('lat', 'lon')
- grad_tokens: bfloat16 [24, 256, 512], P('lat', 'lon')
- grad_qkv: float32 [512, 1536], P('lat')
- grad_out: float32 [512, 512], P('lat')
- grad_up: float32 [512, 1024], P('lat')
- grad_down: float32 [1024, 512], P('lat')
The draws below stay inside these ranges and needn't reach their ends.
Inputs may be any that keep to these rules, and one draw needn't show every extreme that they name: The ocean patches of row r in sector s are that sector's first ocean_count[r, s] positions; the others are land.
All inputs are finite; a program needn't handle non-finite values.
Results may differ from the reference program's by a relative error of at most 0.023.
Values may be sent and summed in bfloat16 or wider, within the bound.
A program may use at most 64 MiB of HBM per device.

```python
import math
import jax
import jax.numpy as jnp
from jax import lax

D = 512
FF = 1024
HEAD_DIM = 64
LON_DEV = 64
ROWS = 24
LON = 256
N_LON = 4


def plant(values, own_key, smallest, largest):
    longest = values.shape.index(max(values.shape))
    spots = []
    for shift in (0, 1):
        where = [jax.random.randint(jax.random.fold_in(own_key, axis), (), 0, length) for axis, length in enumerate(values.shape)]
        where[longest] = (where[longest] + shift) % values.shape[longest]
        spots.append(tuple(where))
    return values.at[spots[0]].set(smallest).at[spots[1]].set(largest)


def shard_levels(rng, extent, pieces, smallest, high):
    def one(position, parts):
        draws = jax.random.uniform(jax.random.fold_in(jax.random.fold_in(rng, 6), position), (parts,), jnp.float32, smallest / len(pieces), high / len(pieces))
        return jnp.repeat(jnp.exp(draws), extent[position] // parts).reshape((-1,) + (1,) * (len(extent) - position - 1))

    level = one(*pieces[0])
    for cut in pieces[1:]:
        level = level * one(*cut)
    return level


def normal_values(stream_key, shape, width, most, split=(), held_as=jnp.bfloat16):
    gain = shard_levels(stream_key, shape, split, -0.22, 0.18) if split else 1.0
    result = jax.random.normal(stream_key, shape, jnp.float32) * width * gain
    return jnp.minimum(jnp.maximum(result, -most), most).astype(held_as)


def setup_inputs(seed: int = 0) -> dict:
    splits = jax.random.split(jax.random.key(seed), 8)
    return {
        "tokens": normal_values(splits[0], (ROWS, LON, D), 1.0, 6.0, ((0, 8), (1, 4))),
        "ocean_count": plant(jax.random.randint(splits[1], (ROWS, N_LON), 1, LON_DEV + 1), jax.random.fold_in(splits[1], 1), 1, LON_DEV).astype(jnp.int32),
        "w_qkv": normal_values(splits[2], (D, 3 * D), D ** -0.5, 0.25),
        "w_out": normal_values(splits[3], (D, D), D ** -0.5, 0.25),
        "w_up": normal_values(splits[4], (D, FF), D ** -0.5, 0.25),
        "w_down": normal_values(splits[5], (FF, D), FF ** -0.5, 0.1875),
        "cotangent": normal_values(splits[6], (ROWS, LON, D), 1.0, 6.0, ((0, 8), (1, 4))),
    }


SOFTMAX_SCALE = 8.0

def widen(values):
    return lax.optimization_barrier(values).astype(jnp.float32)

def elementwise_product(pattern, left_side, right_side):
    return jnp.einsum(pattern, widen(left_side), widen(right_side), precision=lax.Precision.HIGHEST)

def flatten(values):
    return values.reshape(-1, values.shape[-1])

def layer_norm(values):
    average = lax.optimization_barrier(jnp.mean(values, axis=-1, keepdims=True))
    centered = values - average
    variance = lax.optimization_barrier(jnp.mean(centered * centered, axis=-1, keepdims=True))
    return centered * lax.rsqrt(variance + 1e-05)

def split_heads(values, head_count):
    return values.reshape(values.shape[:-1] + (head_count, values.shape[-1] // head_count))

def head_norm(values, head_count):
    shaped = split_heads(values, head_count)
    scaled = shaped * lax.rsqrt(lax.optimization_barrier(jnp.mean(shaped * shaped, axis=-1, keepdims=True)) + 1e-06)
    return scaled.reshape(values.shape)

def project_in(tokens, w_qkv, head_count):
    model_width = tokens.shape[-1]
    normed = layer_norm(tokens.astype(jnp.float32)).astype(jnp.bfloat16)
    projected = elementwise_product('...d,de->...e', normed, w_qkv)
    query_raw = projected[..., :model_width]
    key_raw = projected[..., model_width:2 * model_width]
    query_b = head_norm(query_raw, head_count).astype(jnp.bfloat16)
    key_value = jnp.concatenate([head_norm(key_raw, head_count), projected[..., 2 * model_width:]], axis=-1).astype(jnp.bfloat16)
    return (normed, query_b, key_value, query_raw, key_raw)

def row_scores(query_b, key_value, key_land_mask, head_count):
    model_width = query_b.shape[-1]
    head_features = model_width // head_count
    query_per_head = split_heads(query_b, head_count)
    key_per_head = split_heads(key_value[:, :model_width], head_count)
    unmasked_logits = elementwise_product('mvp,lvp->vml', query_per_head, key_per_head) * (SOFTMAX_SCALE / head_features)
    return jnp.exp(unmasked_logits - SOFTMAX_SCALE) * key_land_mask.astype(jnp.float32)[None, None, :]

def attend_row(query_b, key_value, key_land_mask, head_count):
    model_width = query_b.shape[-1]
    expscore = row_scores(query_b, key_value, key_land_mask, head_count)
    value_heads = split_heads(key_value[:, model_width:], head_count)
    numerator = elementwise_product('hqk,khc->qhc', expscore.astype(jnp.bfloat16), value_heads)
    row_total = jnp.transpose(lax.optimization_barrier(jnp.sum(expscore, axis=-1)))
    return (numerator.reshape(numerator.shape[0], model_width), row_total)

def attend_row_back(query_b, key_value, key_land_mask, row_total, grad_b, gradient_correction, head_count):
    model_width = query_b.shape[-1]
    head_features = model_width // head_count
    expscore = row_scores(query_b, key_value, key_land_mask, head_count)
    row_attention_weight = expscore / jnp.transpose(row_total)[:, :, None]
    query_per_head = split_heads(query_b, head_count)
    key_per_head = split_heads(key_value[:, :model_width], head_count)
    value_heads = split_heads(key_value[:, model_width:], head_count)
    grad_heads = split_heads(grad_b, head_count)
    gradient_weights = elementwise_product('mvp,lvp->vml', grad_heads, value_heads)
    gradient_logits = (row_attention_weight * (gradient_weights - jnp.transpose(gradient_correction)[:, :, None]) * (SOFTMAX_SCALE / head_features)).astype(jnp.bfloat16)
    grad_query = elementwise_product('hqk,khc->qhc', gradient_logits, key_per_head).reshape(-1, model_width)
    grad_key = elementwise_product('hqk,qhc->khc', gradient_logits, query_per_head).reshape(-1, model_width)
    grad_value = elementwise_product('hqk,qhc->khc', row_attention_weight.astype(jnp.bfloat16), grad_heads).reshape(-1, model_width)
    return (grad_query, jnp.concatenate([grad_key, grad_value], axis=-1))

def forward_tail(tokens, attended_b, ocean_mask, w_out, w_up, w_down):
    middle = tokens.astype(jnp.float32) + ocean_mask[..., None] * elementwise_product('...d,de->...e', attended_b, w_out)
    normed_two = layer_norm(middle).astype(jnp.bfloat16)
    lifted = elementwise_product('...d,df->...f', normed_two, w_up)
    active = jax.nn.gelu(lifted).astype(jnp.bfloat16)
    block_out = (middle + ocean_mask[..., None] * elementwise_product('...f,fd->...d', active, w_down)).astype(jnp.bfloat16)
    return (block_out, (middle, normed_two, lifted, active))

def backward_tail(cotangent, ocean_mask, attended_b, tail_saved, w_out, w_up, w_down):
    middle, normed_two, lifted, active = tail_saved
    upstream = cotangent.astype(jnp.float32)
    grad_branch = (ocean_mask[..., None] * upstream).astype(jnp.bfloat16)
    grad_active = elementwise_product('...d,fd->...f', grad_branch, w_down)
    grad_lifted = jax.vjp(jax.nn.gelu, lifted)[1](grad_active)[0].astype(jnp.bfloat16)
    grad_normed = elementwise_product('...f,df->...d', grad_lifted, w_up)
    grad_middle = upstream + jax.vjp(layer_norm, middle)[1](grad_normed)[0]
    grad_attn = (ocean_mask[..., None] * grad_middle).astype(jnp.bfloat16)
    grad_attended = elementwise_product('...e,de->...d', grad_attn, w_out).astype(jnp.bfloat16)
    term_out = elementwise_product('td,te->de', flatten(attended_b), flatten(grad_attn))
    term_up = elementwise_product('td,tf->df', flatten(normed_two), flatten(grad_lifted))
    term_down = elementwise_product('tf,td->fd', flatten(active), flatten(grad_branch))
    return (grad_middle, grad_attended, (term_out, term_up, term_down))

def backward_head(tokens, normed, query_raw, key_raw, grad_query, grad_kv, grad_middle, w_qkv, head_count):
    model_width = tokens.shape[-1]
    grad_qraw = jax.vjp(lambda values: head_norm(values, head_count), query_raw)[1](grad_query)[0]
    grad_kraw = jax.vjp(lambda values: head_norm(values, head_count), key_raw)[1](grad_kv[..., :model_width])[0]
    grad_projected = jnp.concatenate([grad_qraw, grad_kraw, grad_kv[..., model_width:]], axis=-1).astype(jnp.bfloat16)
    term_qkv = elementwise_product('td,te->de', flatten(normed), flatten(grad_projected))
    grad_normed = elementwise_product('...e,de->...d', grad_projected, w_qkv)
    grad_layer = jax.vjp(layer_norm, tokens.astype(jnp.float32))[1](grad_normed)[0]
    return ((grad_middle + grad_layer).astype(jnp.bfloat16), term_qkv)

def reference(tokens, ocean_count, w_qkv, w_out, w_up, w_down, cotangent):
    head_count = D // HEAD_DIM
    positions = jnp.arange(LON, dtype=jnp.int32)
    grad_scale = 1.0 / math.sqrt(ROWS * LON)

    def one_row(weight_sums, row_inputs):
        row_tokens, row_count, row_grad = row_inputs
        sector_count = jnp.take(row_count, (positions // LON_DEV).astype(jnp.int32))
        ocean_mask = (positions % LON_DEV < sector_count).astype(jnp.float32)
        key_land_mask = ocean_mask.astype(jnp.bfloat16)
        normed, query_b, key_value, query_raw, key_raw = project_in(row_tokens, w_qkv, head_count)
        numerator, row_total = attend_row(query_b, key_value, key_land_mask, head_count)
        attended = (split_heads(numerator, head_count) / row_total[:, :, None]).reshape(LON, D)
        attended_b = attended.astype(jnp.bfloat16)
        block_row, tail_saved = forward_tail(row_tokens, attended_b, ocean_mask, w_out, w_up, w_down)
        grad_middle, grad_attended, tail_terms = backward_tail(row_grad, ocean_mask, attended_b, tail_saved, w_out, w_up, w_down)
        gradient_correction = lax.optimization_barrier(jnp.sum(split_heads(widen(grad_attended) * attended, head_count), axis=-1))
        query_parts = []
        grad_kv = jnp.zeros((LON, 2 * D), jnp.float32)
        for sector in range(N_LON):
            first_pos = sector * LON_DEV
            part_query, part_kv = attend_row_back(query_b[first_pos:first_pos + LON_DEV], key_value, key_land_mask, row_total[first_pos:first_pos + LON_DEV], grad_attended[first_pos:first_pos + LON_DEV], gradient_correction[first_pos:first_pos + LON_DEV], head_count)
            query_parts.append(part_query)
            grad_kv = grad_kv + widen(part_kv.astype(jnp.bfloat16))
        grad_query = jnp.concatenate(query_parts, axis=0)
        grad_row, term_qkv = backward_head(row_tokens, normed, query_raw, key_raw, grad_query, grad_kv, grad_middle, w_qkv, head_count)
        new_sums = (weight_sums[0] + term_qkv, weight_sums[1] + tail_terms[0], weight_sums[2] + tail_terms[1], weight_sums[3] + tail_terms[2])
        return (new_sums, (block_row, grad_row))
    start_sums = (jnp.zeros((D, 3 * D), jnp.float32), jnp.zeros((D, D), jnp.float32), jnp.zeros((D, FF), jnp.float32), jnp.zeros((FF, D), jnp.float32))
    weight_sums, row_outputs = lax.scan(one_row, start_sums, (tokens, ocean_count, cotangent))
    block_out, grad_tokens = row_outputs
    return (block_out, grad_tokens, weight_sums[0] * grad_scale, weight_sums[1] * grad_scale, weight_sums[2] * grad_scale, weight_sums[3] * grad_scale)
```

```python
import functools
import math

import jax
import jax.numpy as jnp
from jax import lax
from jax.experimental import pallas as pl
from jax.experimental.pallas import tpu as pltpu
from jax.sharding import PartitionSpec as P

HEAD_DIM = 64
SECTORS = 4
QUAD = 4 * HEAD_DIM
LANES = 128
MESH = pl.DeviceIdType.MESH
F32 = jnp.float32
BF16 = jnp.bfloat16


def nn(a, b):
    return jnp.dot(a, b, preferred_element_type=F32)


def nt(a, b):
    return lax.dot_general(a, b, (((1,), (1,)), ((), ())), preferred_element_type=F32)


def tn(a, b):
    return lax.dot_general(a, b, (((0,), (0,)), ((), ())), preferred_element_type=F32)


def split_two(values):
    high = values.astype(BF16)
    return high, (values - high.astype(F32)).astype(BF16)


def norm_stats(values):
    average = jnp.mean(values, axis=-1, keepdims=True)
    centered = values - average
    variance = jnp.mean(centered * centered, axis=-1, keepdims=True)
    inverse = lax.rsqrt(variance + 1e-05)
    return centered * inverse, inverse


def norm_back(grad, normed, inverse):
    first = jnp.mean(grad, axis=-1, keepdims=True)
    second = jnp.mean(grad * normed, axis=-1, keepdims=True)
    return inverse * (grad - first - normed * second)


def head_mean(values, blocks):
    parts = []
    for start in range(0, values.shape[1], QUAD):
        high, low = split_two(values[:, start : start + QUAD])
        parts.append(nn(high, blocks) + nn(low, blocks))
    return jnp.concatenate(parts, axis=1)


def kernel(lat_n, scale, *refs):
    x_ref, cot_ref, wqkv, wout, wup, wdown = refs[:6]
    bo_ref, gt_ref, gqkv, gout, gup, gdown = refs[6:12]
    xg, ka, va, ma, qa, probs, att_ref, ivb_ref, dq_ref, dk_ref, dv_ref, gaall, stats = refs[12:25]
    own_sem_s, own_sem_r, lat_s, lat_r, all_s, all_r = refs[25:31]
    bufs = refs[31:]
    rows, length, wide = x_ref.shape
    width = wide - LANES
    count = rows * length
    quads = width // QUAD

    lat = lax.axis_index("lat")
    lon = lax.axis_index("lon")
    x_pos, core = lon // 2, lon % 2
    core_peer = (lat, x_pos * 2 + (1 - core))
    x_peer = (lat, (1 - x_pos) * 2 + core)
    far_peer = (lat, (1 - x_pos) * 2 + (1 - core))

    barrier = pltpu.get_barrier_semaphore()
    for peer in (core_peer, x_peer, far_peer):
        pl.semaphore_signal(barrier, inc=1, device_id=peer, device_id_type=MESH)

    @pl.loop(1, lat_n)
    def _(offset):
        pl.semaphore_signal(
            barrier, inc=1, device_id=(lax.rem(lat + offset, lat_n), lon), device_id_type=MESH
        )

    pl.semaphore_wait(barrier, 3 + lat_n - 1)

    def remote(src, dst, send, recv, peer):
        return pltpu.make_async_remote_copy(
            src_ref=src, dst_ref=dst, send_sem=send, recv_sem=recv,
            device_id=peer, device_id_type=MESH,
        )

    def gather(src, buf, base):
        near = remote(src, buf.at[1], own_sem_s.at[base], own_sem_r.at[base], core_peer)
        across = remote(src, buf.at[2], own_sem_s.at[base + 1], own_sem_r.at[base + 1], x_peer)
        onward = remote(
            buf.at[2], buf.at[3], own_sem_s.at[base + 2], own_sem_r.at[base + 2], core_peer
        )
        across.start()
        near.start()
        return near, across, onward

    x_near, x_across, x_onward = gather(x_ref, xg, 0)

    lane = lax.broadcasted_iota(jnp.int32, (1, QUAD), 1) // HEAD_DIM
    lane_f = [jnp.where(lane == h, 1.0, 0.0).astype(F32) for h in range(4)]
    lane_b = [m.astype(BF16) for m in lane_f]
    blocks = jnp.where(
        lax.broadcasted_iota(jnp.int32, (QUAD, QUAD), 0) // HEAD_DIM
        == lax.broadcasted_iota(jnp.int32, (QUAD, QUAD), 1) // HEAD_DIM,
        1.0 / HEAD_DIM,
        0.0,
    ).astype(BF16)
    heads = width // HEAD_DIM
    head_row = lax.broadcasted_iota(jnp.int32, (heads, width), 0)
    head_col = lax.broadcasted_iota(jnp.int32, (heads, width), 1)
    pick_sum = jnp.where(head_col // HEAD_DIM == head_row, 1.0, 0.0).astype(BF16)
    pick_one = jnp.where(head_col == head_row * HEAD_DIM, 1.0, 0.0).astype(BF16)

    def stack(tile):
        return jnp.concatenate([tile * lane_b[h] for h in range(4)], axis=0)

    def combine(tile):
        total = tile[:HEAD_DIM] * lane_f[0]
        for h in range(1, 4):
            total = total + tile[h * length : (h + 1) * length] * lane_f[h]
        return total

    def per_row(values):
        return values.reshape(rows, length, values.shape[-1])

    def project(slot):
        block = (x_ref[...] if slot == 0 else xg[slot]).reshape(count, wide)
        mask = block[:, width:]
        mask_wide = jnp.concatenate([mask.astype(F32)] * (width // LANES), axis=1)
        normed, inverse = norm_stats(block[:, :width].astype(F32))
        normed_b = normed.astype(BF16)
        query_raw = nn(normed_b, wqkv[:, :width])
        key_raw = nn(normed_b, wqkv[:, width : 2 * width])
        value = nn(normed_b, wqkv[:, 2 * width :])
        q_inv = lax.rsqrt(head_mean(query_raw * query_raw, blocks) + 1e-06)
        k_inv = lax.rsqrt(head_mean(key_raw * key_raw, blocks) + 1e-06)
        at = pl.ds(slot * length, length)
        qa[:, at, :] = per_row((query_raw * q_inv).astype(BF16))
        ka[:, at, :] = per_row((key_raw * k_inv * mask_wide).astype(BF16))
        va[:, at, :] = per_row((value * mask_wide).astype(BF16))
        ma[:, at, :] = per_row(mask)
        return normed, inverse, normed_b, query_raw, key_raw, q_inv, k_inv, mask_wide

    normed, inverse, normed_b, query_raw, key_raw, q_inv, k_inv, mask_wide = project(0)
    x_near.wait_recv()
    project(1)
    x_across.wait_recv()
    x_onward.start()
    project(2)
    x_onward.wait_recv()
    project(3)
    for copy in (x_near, x_across, x_onward):
        copy.wait_send()

    logit = 8.0 / HEAD_DIM

    @pl.loop(0, rows)
    def _(r):
        for qd in range(quads):
            cs = slice(qd * QUAD, (qd + 1) * QUAD)
            key, value = ka[r, :, cs], va[r, :, cs]
            score = jnp.exp(nt(stack(qa[r, 0:length, cs]), key) * logit - 8.0)
            score_b = score.astype(BF16)
            part = 1.0 / nn(score_b, ma[r])
            part = jnp.concatenate([part, part], axis=1)
            probs[r, qd] = score * part
            att_ref[r, :, cs] = combine(nn(score_b, value) * part)
            ivb_ref[r, :, cs] = combine(part)

    tokens = x_ref[...].reshape(count, wide)[:, :width].astype(F32)
    cotangent = cot_ref[...].reshape(count, width).astype(F32)
    attended = att_ref[...].reshape(count, width)
    attended_b = attended.astype(BF16)
    middle = tokens + mask_wide * nn(attended_b, wout[...])
    normed_two, inverse_two = norm_stats(middle)
    normed_two_b = normed_two.astype(BF16)
    lifted = nn(normed_two_b, wup[...])
    root = math.sqrt(2.0 / math.pi)
    square = lifted * lifted
    curve = jnp.tanh(root * lifted * (1.0 + 0.044715 * square))
    half = 0.5 * (1.0 + curve)
    active = (lifted * half).astype(BF16)
    slope = half + 0.5 * lifted * (1.0 - curve * curve) * (root * (1.0 + 3 * 0.044715 * square))
    bo_ref[...] = per_row((middle + mask_wide * nn(active, wdown[...])).astype(BF16))

    grad_branch = (mask_wide * cotangent).astype(BF16)
    grad_lifted = (slope * nt(grad_branch, wdown[...])).astype(BF16)
    grad_middle = cotangent + norm_back(nt(grad_lifted, wup[...]), normed_two, inverse_two)
    grad_attn = (mask_wide * grad_middle).astype(BF16)
    grad_attended = nt(grad_attn, wout[...]).astype(BF16)
    gaall[0] = per_row(grad_attended)
    product = per_row(grad_attended.astype(F32) * attended)
    for r in range(rows):
        high, low = split_two(ivb_ref[r])
        part = nt(pick_one, high) + nt(pick_one, low)
        high, low = split_two(product[r])
        delta = nt(pick_sum, high) + nt(pick_sum, low)
        pair = jnp.concatenate([part, delta], axis=0)
        stats[0, r] = jnp.concatenate([pair, jnp.zeros_like(pair)], axis=1)

    g_near, g_across, g_onward = gather(gaall.at[0], gaall, 3)
    s_near, s_across, s_onward = gather(stats.at[0], stats, 6)

    pending = {}

    def begin(c, left, right):
        part, from_core, to_x, from_x, total, from_lat, mine, everyone = bufs[8 * c : 8 * c + 8]
        _, _, n, r, c4 = part.shape
        full = tn(left, right) * scale
        for l in range(SECTORS):
            part[l % 2, l // 2] = full[:, l * c4 : (l + 1) * c4].reshape(n, r, c4).astype(BF16)
        base = 9 + 5 * c
        copy = remote(
            part.at[1 - core], from_core, own_sem_s.at[base], own_sem_r.at[base], core_peer
        )
        copy.start()
        pending[c] = copy

    def pass_x(c):
        part, from_core, to_x, from_x, total, from_lat, mine, everyone = bufs[8 * c : 8 * c + 8]
        pending[c].wait()
        other = 1 - x_pos
        to_x[...] = (
            part[core, other].astype(F32) + from_core[other].astype(F32)
        ).astype(BF16)
        base = 9 + 5 * c + 1
        copy = remote(to_x, from_x, own_sem_s.at[base], own_sem_r.at[base], x_peer)
        copy.start()
        pending[c] = copy

    def lat_copy(c, offset):
        total, from_lat = bufs[8 * c + 4], bufs[8 * c + 5]
        target = lax.rem(lat + offset, lat_n)
        return remote(
            total.at[target], from_lat.at[offset - 1],
            lat_s.at[c, offset - 1], lat_r.at[c, offset - 1], (target, lon),
        )

    def pass_lat(c):
        part, from_core, to_x, from_x, total, from_lat, mine, everyone = bufs[8 * c : 8 * c + 8]
        pending[c].wait()
        total[...] = (
            part[core, x_pos].astype(F32) + from_core[x_pos].astype(F32) + from_x[...].astype(F32)
        ).astype(BF16)

        @pl.loop(1, lat_n)
        def _(offset):
            lat_copy(c, offset).start()

    def pass_lon(c):
        part, from_core, to_x, from_x, total, from_lat, mine, everyone = bufs[8 * c : 8 * c + 8]

        @pl.loop(1, lat_n)
        def _(offset):
            lat_copy(c, offset).wait()

        everyone[lon] = (
            total[lat].astype(F32) + jnp.sum(from_lat[...].astype(F32), axis=0)
        ).astype(BF16)
        copies = []
        for i, peer in enumerate((x_peer, far_peer, core_peer)):
            copy = remote(
                everyone.at[lon], everyone.at[lon], all_s.at[c, i], all_r.at[c, i], peer
            )
            copy.start()
            copies.append(copy)
        pending[c] = copies

    def finish(c, out, first):
        everyone = bufs[8 * c + 7]
        c4 = everyone.shape[-1]
        for copy in pending[c]:
            copy.wait()
        for l in range(SECTORS):
            out[:, first + l * c4 : first + (l + 1) * c4] = everyone[l].astype(F32)

    begin(0, active, grad_branch)
    begin(1, normed_two_b, grad_lifted)
    pass_x(0)
    begin(2, attended_b, grad_attn)

    @pl.loop(0, rows)
    def _(r):
        for qd in range(quads):
            cs = slice(qd * QUAD, (qd + 1) * QUAD)
            key, value = ka[r, :, cs], va[r, :, cs]
            tall = stack(gaall[0, r, :, cs])
            delta = jnp.sum(
                tall.astype(F32) * jnp.concatenate([att_ref[r, :, cs]] * 4, axis=0),
                axis=-1,
                keepdims=True,
            )
            back = (probs[r, qd] * (nt(tall, value) - delta) * logit).astype(BF16)
            dq_ref[r, :, cs] = combine(nn(back, key))

    def head_back(grad, raw, inv):
        return inv * (grad - raw * (inv * inv) * head_mean(raw * grad, blocks))

    g_across.wait_recv()
    g_onward.start()
    s_across.wait_recv()
    s_onward.start()
    pass_x(1)
    grad_q = head_back(dq_ref[...].reshape(count, width), query_raw, q_inv).astype(BF16)
    begin(3, normed_b, grad_q)
    pass_x(2)
    pass_lat(0)
    for copy in (g_near, s_near, g_onward, s_onward):
        copy.wait_recv()

    @pl.loop(0, rows)
    def _(r):
        stat = jnp.concatenate([stats[s, r][:, :length] for s in range(SECTORS)], axis=1)
        for qd in range(quads):
            cs = slice(qd * QUAD, (qd + 1) * QUAD)
            query = qa[r, :, cs]
            grad = jnp.concatenate([gaall[s, r, :, cs] for s in range(SECTORS)], axis=0)

            def spread(base):
                return jnp.concatenate(
                    [
                        jnp.broadcast_to(stat[base + h : base + h + 1], (length, QUAD))
                        for h in range(qd * 4, qd * 4 + 4)
                    ],
                    axis=0,
                )

            score = jnp.exp(nt(stack(ka[r, 0:length, cs]), query) * logit - 8.0) * spread(0)
            deep = nt(stack(va[r, 0:length, cs]), grad)
            back = (score * (deep - spread(heads)) * logit).astype(BF16)
            dk_ref[r, :, cs] = combine(nn(back, query))
            dv_ref[r, :, cs] = combine(nn(score.astype(BF16), grad))

    pass_x(3)
    pass_lat(1)
    grad_k = head_back(
        dk_ref[...].reshape(count, width) * mask_wide, key_raw, k_inv
    ).astype(BF16)
    grad_v = (dv_ref[...].reshape(count, width) * mask_wide).astype(BF16)
    grad_kv = jnp.concatenate([grad_k, grad_v], axis=1)
    begin(4, normed_b, grad_kv)
    pass_lat(2)
    pass_lon(0)
    pass_x(4)
    grad_normed = (
        nt(grad_q, wqkv[:, :width])
        + nt(grad_k, wqkv[:, width : 2 * width])
        + nt(grad_v, wqkv[:, 2 * width :])
    )
    gt_ref[...] = per_row((grad_middle + norm_back(grad_normed, normed, inverse)).astype(BF16))
    pass_lat(3)
    pass_lon(1)
    finish(0, gdown, 0)
    pass_lon(2)
    finish(1, gup, 0)
    pass_lat(4)
    pass_lon(3)
    finish(2, gout, 0)
    finish(3, gqkv, 0)
    for copy in (g_near, g_across, g_onward, s_near, s_across, s_onward):
        copy.wait_send()
    pass_lon(4)
    finish(4, gqkv, width)


def local(lat_n, tokens, ocean_count, w_qkv, w_out, w_up, w_down, cotangent):
    rows, length, width = tokens.shape
    heads = width // HEAD_DIM
    hidden = w_up.shape[1]
    lon_n = SECTORS
    mask = (
        lax.broadcasted_iota(jnp.int32, (rows, length, LANES), 1) < ocean_count[:, :, None]
    ).astype(BF16)
    extended = jnp.concatenate([tokens, mask], axis=-1)
    scale = 1.0 / math.sqrt(rows * lat_n * length * lon_n)
    quads = width // QUAD
    full = length * SECTORS
    scratch = [
        pltpu.VMEM((SECTORS, rows, length, width + LANES), BF16),
        pltpu.VMEM((rows, full, width), BF16),
        pltpu.VMEM((rows, full, width), BF16),
        pltpu.VMEM((rows, full, LANES), BF16),
        pltpu.VMEM((rows, full, width), BF16),
        pltpu.VMEM((rows, quads, 4 * length, full), F32),
        pltpu.VMEM((rows, length, width), F32),
        pltpu.VMEM((rows, length, width), F32),
        pltpu.VMEM((rows, length, width), F32),
        pltpu.VMEM((rows, length, width), F32),
        pltpu.VMEM((rows, length, width), F32),
        pltpu.VMEM((SECTORS, rows, length, width), BF16),
        pltpu.VMEM((SECTORS, rows, 2 * heads, LANES), F32),
        pltpu.SemaphoreType.DMA((34,)),
        pltpu.SemaphoreType.DMA((34,)),
        pltpu.SemaphoreType.DMA((5, lat_n - 1)),
        pltpu.SemaphoreType.DMA((5, lat_n - 1)),
        pltpu.SemaphoreType.DMA((5, 3)),
        pltpu.SemaphoreType.DMA((5, 3)),
    ]
    for tall, broad in (
        (hidden, width), (width, hidden), (width, width), (width, width), (width, 2 * width)
    ):
        r, c4 = tall // lat_n, broad // SECTORS
        scratch += [
            pltpu.VMEM((2, 2, lat_n, r, c4), BF16),
            pltpu.VMEM((2, lat_n, r, c4), BF16),
            pltpu.VMEM((lat_n, r, c4), BF16),
            pltpu.VMEM((lat_n, r, c4), BF16),
            pltpu.VMEM((lat_n, r, c4), BF16),
            pltpu.VMEM((lat_n - 1, r, c4), BF16),
            pltpu.VMEM((8, LANES), BF16),
            pltpu.VMEM((SECTORS, r, c4), BF16),
        ]
    vmem = pl.BlockSpec(memory_space=pltpu.VMEM)
    return pl.pallas_call(
        functools.partial(kernel, lat_n, scale),
        out_shape=(
            jax.ShapeDtypeStruct(tokens.shape, BF16),
            jax.ShapeDtypeStruct(tokens.shape, BF16),
            jax.ShapeDtypeStruct((width // lat_n, 3 * width), F32),
            jax.ShapeDtypeStruct((width // lat_n, width), F32),
            jax.ShapeDtypeStruct((width // lat_n, hidden), F32),
            jax.ShapeDtypeStruct((hidden // lat_n, width), F32),
        ),
        in_specs=[vmem] * 6,
        out_specs=(vmem,) * 6,
        scratch_shapes=scratch,
        compiler_params=pltpu.CompilerParams(
            collective_id=0, has_side_effects=True, vmem_limit_bytes=56 * 1024 * 1024
        ),
    )(extended, cotangent, w_qkv, w_out, w_up, w_down)


def solution(mesh):
    rows = P("lat", "lon", None)
    in_specs = (rows, P("lat", "lon"), P(), P(), P(), P(), rows)
    out_specs = (rows, rows, P("lat", None), P("lat", None), P("lat", None), P("lat", None))
    return jax.shard_map(
        functools.partial(local, mesh.shape["lat"]),
        mesh=mesh,
        in_specs=in_specs,
        out_specs=out_specs,
        check_vma=False,
    )
```

```python
import functools
import math

import jax
import jax.numpy as jnp
from jax import lax
from jax.experimental import pallas as pl
from jax.experimental.pallas import tpu as pltpu
from jax.sharding import PartitionSpec as P

HEAD_DIM = 64
SECTORS = 4
QUAD = 4 * HEAD_DIM
LANES = 128
MESH = pl.DeviceIdType.MESH
F32 = jnp.float32
BF16 = jnp.bfloat16


def nn(a, b):
    return jnp.dot(a, b, preferred_element_type=F32)


def nt(a, b):
    return lax.dot_general(a, b, (((1,), (1,)), ((), ())), preferred_element_type=F32)


def tn(a, b):
    return lax.dot_general(a, b, (((0,), (0,)), ((), ())), preferred_element_type=F32)


def split_two(values):
    high = values.astype(BF16)
    return high, (values - high.astype(F32)).astype(BF16)


def norm_stats(values):
    average = jnp.mean(values, axis=-1, keepdims=True)
    centered = values - average
    variance = jnp.mean(centered * centered, axis=-1, keepdims=True)
    inverse = lax.rsqrt(variance + 1e-05)
    return centered * inverse, inverse


def norm_back(grad, normed, inverse):
    first = jnp.mean(grad, axis=-1, keepdims=True)
    second = jnp.mean(grad * normed, axis=-1, keepdims=True)
    return inverse * (grad - first - normed * second)


def head_mean(values, blocks):
    parts = []
    for start in range(0, values.shape[1], QUAD):
        high, low = split_two(values[:, start : start + QUAD])
        parts.append(nn(high, blocks) + nn(low, blocks))
    return jnp.concatenate(parts, axis=1)


def kernel(lat_n, scale, *refs):
    x_ref, count_ref, cot_hbm, wqkv_hbm, wout_hbm, wup_hbm, wdown_hbm = refs[:7]
    bo_hbm, gt_hbm, gqkv_hbm, gout_hbm, gup_hbm, gdown_hbm = refs[7:13]
    cot_ref, wqkv, wout, wup, wdown = refs[13:18]
    bo_ref, gt_ref, gqkv, gout, gup, gdown = refs[18:24]
    xg, cg, ka, va, ma, qa, probs, att_ref, ivb_ref, dq_ref, dk_ref, dv_ref, gaall, stats = refs[24:38]
    sem_s, sem_r, lat_s, lat_r, all_s, all_r, in_sem, out_sem = refs[38:46]
    bufs = refs[46:]
    rows, length, width = x_ref.shape
    count = rows * length
    quads = width // QUAD
    half_n = lat_n // 2

    lat = lax.axis_index("lat")
    lon = lax.axis_index("lon")
    x_pos, core = lon // 2, lon % 2
    hi, lo = lat // 2, lat % 2
    core_peer = (lat, x_pos * 2 + (1 - core))
    x_peer = (lat, (1 - x_pos) * 2 + core)
    far_peer = (lat, (1 - x_pos) * 2 + (1 - core))
    lo_peer = (hi * 2 + (1 - lo), lon)

    barrier = pltpu.get_barrier_semaphore()
    for peer in (core_peer, x_peer, far_peer, lo_peer):
        pl.semaphore_signal(barrier, inc=1, device_id=peer, device_id_type=MESH)

    def hi_peer(offset):
        return lax.rem(hi + offset, half_n)

    @pl.loop(1, half_n)
    def _(offset):
        pl.semaphore_signal(
            barrier, inc=1, device_id=(hi_peer(offset) * 2 + lo, lon), device_id_type=MESH
        )

    loads = []
    for i, (src, dst) in enumerate(
        ((wqkv_hbm, wqkv), (wout_hbm, wout), (cot_hbm, cot_ref), (wup_hbm, wup), (wdown_hbm, wdown))
    ):
        load = pltpu.make_async_copy(src, dst, in_sem.at[i])
        load.start()
        loads.append(load)

    cg[0] = jnp.zeros_like(cg[0])
    cg[0, 0:rows] = jnp.broadcast_to(count_ref[...], (rows, LANES))
    pl.semaphore_wait(barrier, 4 + half_n - 1)

    def remote(src, dst, send, recv, peer):
        return pltpu.make_async_remote_copy(
            src_ref=src, dst_ref=dst, send_sem=send, recv_sem=recv,
            device_id=peer, device_id_type=MESH,
        )

    def gather(src, buf, base):
        near = remote(src, buf.at[1], sem_s.at[base], sem_r.at[base], core_peer)
        across = remote(src, buf.at[2], sem_s.at[base + 1], sem_r.at[base + 1], x_peer)
        onward = remote(buf.at[2], buf.at[3], sem_s.at[base + 2], sem_r.at[base + 2], core_peer)
        across.start()
        near.start()
        return near, across, onward

    c_near, c_across, c_onward = gather(cg.at[0], cg, 9)
    x_near, x_across, x_onward = gather(x_ref, xg, 0)

    lane = lax.broadcasted_iota(jnp.int32, (1, QUAD), 1) // HEAD_DIM
    lane_f = [jnp.where(lane == h, 1.0, 0.0).astype(F32) for h in range(4)]
    lane_b = [m.astype(BF16) for m in lane_f]
    blocks = jnp.where(
        lax.broadcasted_iota(jnp.int32, (QUAD, QUAD), 0) // HEAD_DIM
        == lax.broadcasted_iota(jnp.int32, (QUAD, QUAD), 1) // HEAD_DIM,
        1.0 / HEAD_DIM,
        0.0,
    ).astype(BF16)
    heads = width // HEAD_DIM
    head_row = lax.broadcasted_iota(jnp.int32, (heads, width), 0)
    head_col = lax.broadcasted_iota(jnp.int32, (heads, width), 1)
    pick_sum = jnp.where(head_col // HEAD_DIM == head_row, 1.0, 0.0).astype(BF16)
    pick_one = jnp.where(head_col == head_row * HEAD_DIM, 1.0, 0.0).astype(BF16)
    place = lax.broadcasted_iota(jnp.int32, (length, LANES), 0)

    def stack(tile):
        return jnp.concatenate([tile * lane_b[h] for h in range(4)], axis=0)

    def combine(tile):
        total = tile[:HEAD_DIM] * lane_f[0]
        for h in range(1, 4):
            total = total + tile[h * length : (h + 1) * length] * lane_f[h]
        return total

    def per_row(values):
        return values.reshape(rows, length, values.shape[-1])

    def unit(raw):
        parts = []
        for start in range(0, width, QUAD):
            piece = raw[:, start : start + QUAD]
            parts.append(nn((piece * piece).astype(BF16), blocks))
        return lax.rsqrt(jnp.concatenate(parts, axis=1) + 1e-06)

    def project_q(slot, normed_b):
        query_raw = nn(normed_b, wqkv[:, :width])
        q_inv = unit(query_raw)
        qa[:, pl.ds(slot * length, length), :] = per_row((query_raw * q_inv).astype(BF16))
        return query_raw, q_inv

    def project_kv(slot):
        block = (x_ref[...] if slot == 0 else xg[slot]).reshape(count, width)
        mask = jnp.concatenate(
            [jnp.where(place < cg[slot, r : r + 1, :], 1.0, 0.0) for r in range(rows)], axis=0
        )
        mask_wide = jnp.concatenate([mask] * (width // LANES), axis=1)
        normed, inverse = norm_stats(block.astype(F32))
        normed_b = normed.astype(BF16)
        if slot == 0:
            loads[0].wait()
        key_raw = nn(normed_b, wqkv[:, width : 2 * width])
        value = nn(normed_b, wqkv[:, 2 * width :])
        k_inv = unit(key_raw)
        at = pl.ds(slot * length, length)
        ka[:, at, :] = per_row((key_raw * k_inv * mask_wide).astype(BF16))
        va[:, at, :] = per_row((value * mask_wide).astype(BF16))
        ma[:, at, :] = per_row(mask.astype(BF16))
        return normed, inverse, normed_b, key_raw, k_inv, mask_wide

    normed, inverse, normed_b, key_raw, k_inv, mask_wide = project_kv(0)
    query_raw, q_inv = project_q(0, normed_b)
    c_across.wait_recv()
    c_onward.start()
    c_near.wait_recv()
    x_near.wait_recv()
    normed_near = project_kv(1)[2]
    x_across.wait_recv()
    x_onward.start()
    normed_across = project_kv(2)[2]
    c_onward.wait_recv()
    x_onward.wait_recv()
    normed_far = project_kv(3)[2]

    logit = 8.0 / HEAD_DIM

    @pl.loop(0, rows)
    def _(r):
        for qd in range(quads):
            cs = slice(qd * QUAD, (qd + 1) * QUAD)
            key, value = ka[r, :, cs], va[r, :, cs]
            score = jnp.exp(nt(stack(qa[r, 0:length, cs]), key) * logit - 8.0)
            score_b = score.astype(BF16)
            part = 1.0 / nn(score_b, ma[r])
            part = jnp.concatenate([part, part], axis=1)
            probs[r, qd] = score * part
            att_ref[r, :, cs] = combine(nn(score_b, value) * part)
            ivb_ref[r, :, cs] = combine(part)

    pending = {}

    def order(c):
        near = (x_pos, lo, x_peer, lo_peer) if c == 5 else (lo, x_pos, lo_peer, x_peer)
        return near

    def chunk(c):
        return bufs[9 * c : 9 * c + 9]

    def begin(c, left, right):
        part, from_core = chunk(c)[:2]
        n, r, c4 = part.shape[-3:]
        full = tn(left, right) * scale
        for l in range(SECTORS):
            piece = full[:, l * c4 : (l + 1) * c4].reshape(n, 2, r, c4).astype(BF16)
            for low in range(2):
                where = (l // 2, low) if c == 5 else (low, l // 2)
                part[(l % 2,) + where] = piece[:, low]
        at = 12 + 3 * c
        copy = remote(part.at[1 - core], from_core, sem_s.at[at], sem_r.at[at], core_peer)
        copy.start()
        pending[c] = copy

    def add(*terms):
        total = terms[0].astype(F32)
        for term in terms[1:]:
            total = total + term.astype(F32)
        return total.astype(BF16)

    def second(c):
        part, from_core, to_one, from_one = chunk(c)[:4]
        first_pos, _, first_peer, _ = order(c)
        pending[c].wait()
        to_one[...] = add(part[core, 1 - first_pos], from_core[1 - first_pos])
        at = 12 + 3 * c + 1
        copy = remote(to_one, from_one, sem_s.at[at], sem_r.at[at], first_peer)
        copy.start()
        pending[c] = copy

    def third(c):
        part, from_core, _, from_one, to_two, from_two = chunk(c)[:6]
        one, two, _, peer = order(c)
        pending[c].wait()
        to_two[...] = add(part[core, one, 1 - two], from_core[one, 1 - two], from_one[1 - two])
        at = 12 + 3 * c + 2
        copy = remote(to_two, from_two, sem_s.at[at], sem_r.at[at], peer)
        copy.start()
        pending[c] = copy

    def lat_copy(c, offset):
        total, from_lat = chunk(c)[6:8]
        target = hi_peer(offset)
        return remote(
            total.at[target], from_lat.at[offset - 1],
            lat_s.at[c, offset - 1], lat_r.at[c, offset - 1], (target * 2 + lo, lon),
        )

    def fourth(c):
        part, from_core, _, from_one, _, from_two, total, _, _ = chunk(c)
        one, two, _, _ = order(c)
        pending[c].wait()
        total[...] = add(part[core, one, two], from_core[one, two], from_one[two], from_two[...])

        @pl.loop(1, half_n)
        def _(offset):
            lat_copy(c, offset).start()

    def fifth(c):
        total, from_lat, everyone = chunk(c)[6:9]

        @pl.loop(1, half_n)
        def _(offset):
            lat_copy(c, offset).wait()

        everyone[lon] = (
            total[hi].astype(F32) + jnp.sum(from_lat[...].astype(F32), axis=0)
        ).astype(BF16)
        copies = []
        for i, peer in enumerate((x_peer, far_peer, core_peer)):
            copy = remote(
                everyone.at[lon], everyone.at[lon], all_s.at[c, i], all_r.at[c, i], peer
            )
            copy.start()
            copies.append(copy)
        pending[c] = copies

    stores = []

    def store(src, dst):
        copy = pltpu.make_async_copy(src, dst, out_sem.at[len(stores)])
        copy.start()
        stores.append(copy)

    def finish(c, out, first):
        everyone = chunk(c)[8]
        c4 = everyone.shape[-1]
        for copy in pending[c]:
            copy.wait()
        for l in range(SECTORS):
            out[:, first + l * c4 : first + (l + 1) * c4] = everyone[l].astype(F32)

    for load in loads[1:]:
        load.wait()
    tokens = x_ref[...].reshape(count, width).astype(F32)
    cotangent = cot_ref[...].reshape(count, width).astype(F32)
    grad_branch = (mask_wide * cotangent).astype(BF16)
    attended = att_ref[...].reshape(count, width)
    attended_b = attended.astype(BF16)
    middle = tokens + mask_wide * nn(attended_b, wout[...])
    normed_two, inverse_two = norm_stats(middle)
    normed_two_b = normed_two.astype(BF16)
    lifted = nn(normed_two_b, wup[...])
    root = math.sqrt(2.0 / math.pi)
    square = lifted * lifted
    curve = jnp.tanh(root * lifted * (1.0 + 0.044715 * square))
    half = 0.5 * (1.0 + curve)
    active = (lifted * half).astype(BF16)
    slope = half + 0.5 * lifted * (1.0 - curve * curve) * (root * (1.0 + 3 * 0.044715 * square))
    begin(0, active, grad_branch)

    grad_lifted = (slope * nt(grad_branch, wdown[...])).astype(BF16)
    grad_middle = cotangent + norm_back(nt(grad_lifted, wup[...]), normed_two, inverse_two)
    second(0)
    grad_attn = (mask_wide * grad_middle).astype(BF16)
    grad_attended = nt(grad_attn, wout[...]).astype(BF16)
    gaall[0] = per_row(grad_attended)
    g_near, g_across, g_onward = gather(gaall.at[0], gaall, 3)
    product = per_row(grad_attended.astype(F32) * attended)
    for r in range(rows):
        high, low = split_two(ivb_ref[r])
        part = nt(pick_one, high) + nt(pick_one, low)
        high, low = split_two(product[r])
        delta = nt(pick_sum, high) + nt(pick_sum, low)
        pair = jnp.concatenate([part, delta], axis=0)
        stats[0, r] = jnp.concatenate([pair, jnp.zeros_like(pair)], axis=1)
    s_near, s_across, s_onward = gather(stats.at[0], stats, 6)

    begin(1, normed_two_b, grad_lifted)
    begin(2, attended_b, grad_attn)
    third(0)
    second(1)
    bo_ref[...] = per_row((middle + mask_wide * nn(active, wdown[...])).astype(BF16))
    store(bo_ref, bo_hbm)
    project_q(1, normed_near)
    project_q(2, normed_across)
    project_q(3, normed_far)
    second(2)
    g_across.wait_recv()
    g_onward.start()
    s_across.wait_recv()
    s_onward.start()

    @pl.loop(0, rows)
    def _(r):
        for qd in range(quads):
            cs = slice(qd * QUAD, (qd + 1) * QUAD)
            key, value = ka[r, :, cs], va[r, :, cs]
            tall = stack(gaall[0, r, :, cs])
            delta = jnp.sum(
                tall.astype(F32) * jnp.concatenate([att_ref[r, :, cs]] * 4, axis=0),
                axis=-1,
                keepdims=True,
            )
            back = (probs[r, qd] * (nt(tall, value) - delta) * logit).astype(BF16)
            dq_ref[r, :, cs] = combine(nn(back, key))

    def head_back(grad, raw, inv):
        return inv * (grad - raw * (inv * inv) * head_mean(raw * grad, blocks))

    third(1)
    grad_q = head_back(dq_ref[...].reshape(count, width), query_raw, q_inv).astype(BF16)
    begin(3, normed_b, grad_q)
    fourth(0)
    third(2)
    second(3)
    for copy in (g_near, s_near, g_onward, s_onward):
        copy.wait_recv()

    @pl.loop(0, rows)
    def _(r):
        stat = jnp.concatenate([stats[s, r][:, :length] for s in range(SECTORS)], axis=1)
        for qd in range(quads):
            cs = slice(qd * QUAD, (qd + 1) * QUAD)
            query = qa[r, :, cs]
            grad = jnp.concatenate([gaall[s, r, :, cs] for s in range(SECTORS)], axis=0)

            def spread(base):
                return jnp.concatenate(
                    [
                        jnp.broadcast_to(stat[base + h : base + h + 1], (length, QUAD))
                        for h in range(qd * 4, qd * 4 + 4)
                    ],
                    axis=0,
                )

            score = jnp.exp(nt(stack(ka[r, 0:length, cs]), query) * logit - 8.0) * spread(0)
            deep = nt(stack(va[r, 0:length, cs]), grad)
            back = (score * (deep - spread(heads)) * logit).astype(BF16)
            dk_ref[r, :, cs] = combine(nn(back, query))
            dv_ref[r, :, cs] = combine(nn(score.astype(BF16), grad))

    grad_v = (dv_ref[...].reshape(count, width) * mask_wide).astype(BF16)
    begin(4, normed_b, grad_v)
    fourth(1)
    third(3)
    grad_k = head_back(
        dk_ref[...].reshape(count, width) * mask_wide, key_raw, k_inv
    ).astype(BF16)
    begin(5, normed_b, grad_k)
    second(4)
    fourth(2)
    fifth(0)
    second(5)
    grad_normed = (
        nt(grad_q, wqkv[:, :width])
        + nt(grad_k, wqkv[:, width : 2 * width])
        + nt(grad_v, wqkv[:, 2 * width :])
    )
    gt_ref[...] = per_row((grad_middle + norm_back(grad_normed, normed, inverse)).astype(BF16))
    store(gt_ref, gt_hbm)
    third(4)
    fourth(3)
    third(5)
    fifth(1)
    finish(0, gdown, 0)
    store(gdown, gdown_hbm)
    fourth(4)
    fifth(2)
    fourth(5)
    finish(1, gup, 0)
    store(gup, gup_hbm)
    fifth(3)
    fifth(4)
    finish(2, gout, 0)
    store(gout, gout_hbm)
    finish(3, gqkv, 0)
    for group in (
        (g_near, g_across, g_onward), (s_near, s_across, s_onward),
        (x_near, x_across, x_onward), (c_near, c_across, c_onward),
    ):
        for copy in group:
            copy.wait_send()
    fifth(5)
    finish(4, gqkv, 2 * width)
    finish(5, gqkv, width)
    store(gqkv, gqkv_hbm)
    for copy in stores:
        copy.wait()


def hand_over(*refs):
    sems = refs[12]
    copies = [pltpu.make_async_copy(refs[i], refs[6 + i], sems.at[i]) for i in range(6)]
    for copy in copies:
        copy.start()
    for copy in copies:
        copy.wait()


def local(lat_n, tokens, ocean_count, w_qkv, w_out, w_up, w_down, cotangent):
    rows, length, width = tokens.shape
    heads = width // HEAD_DIM
    hidden = w_up.shape[1]
    half_n = lat_n // 2
    scale = 1.0 / math.sqrt(rows * lat_n * length * SECTORS)
    quads = width // QUAD
    full = length * SECTORS
    out_shape = (
        jax.ShapeDtypeStruct(tokens.shape, BF16),
        jax.ShapeDtypeStruct(tokens.shape, BF16),
        jax.ShapeDtypeStruct((width // lat_n, 3 * width), F32),
        jax.ShapeDtypeStruct((width // lat_n, width), F32),
        jax.ShapeDtypeStruct((width // lat_n, hidden), F32),
        jax.ShapeDtypeStruct((hidden // lat_n, width), F32),
    )
    scratch = [pltpu.VMEM(a.shape, BF16) for a in (cotangent, w_qkv, w_out, w_up, w_down)]
    scratch += [pltpu.VMEM(a.shape, a.dtype) for a in out_shape]
    scratch += [
        pltpu.VMEM((SECTORS, rows, length, width), BF16),
        pltpu.VMEM((SECTORS, -(-rows // 8) * 8, LANES), jnp.int32),
        pltpu.VMEM((rows, full, width), BF16),
        pltpu.VMEM((rows, full, width), BF16),
        pltpu.VMEM((rows, full, LANES), BF16),
        pltpu.VMEM((rows, full, width), BF16),
        pltpu.VMEM((rows, quads, 4 * length, full), F32),
        pltpu.VMEM((rows, length, width), F32),
        pltpu.VMEM((rows, length, width), F32),
        pltpu.VMEM((rows, length, width), F32),
        pltpu.VMEM((rows, length, width), F32),
        pltpu.VMEM((rows, length, width), F32),
        pltpu.VMEM((SECTORS, rows, length, width), BF16),
        pltpu.VMEM((SECTORS, rows, 2 * heads, LANES), F32),
        pltpu.SemaphoreType.DMA((30,)),
        pltpu.SemaphoreType.DMA((30,)),
        pltpu.SemaphoreType.DMA((6, half_n - 1)),
        pltpu.SemaphoreType.DMA((6, half_n - 1)),
        pltpu.SemaphoreType.DMA((6, 3)),
        pltpu.SemaphoreType.DMA((6, 3)),
        pltpu.SemaphoreType.DMA((5,)),
        pltpu.SemaphoreType.DMA((6,)),
    ]
    for tall, broad in ((hidden, width), (width, hidden)) + ((width, width),) * 4:
        r, c4 = tall // lat_n, broad // SECTORS
        scratch += [
            pltpu.VMEM((2, 2, 2, half_n, r, c4), BF16),
            pltpu.VMEM((2, 2, half_n, r, c4), BF16),
            pltpu.VMEM((2, half_n, r, c4), BF16),
            pltpu.VMEM((2, half_n, r, c4), BF16),
            pltpu.VMEM((half_n, r, c4), BF16),
            pltpu.VMEM((half_n, r, c4), BF16),
            pltpu.VMEM((half_n, r, c4), BF16),
            pltpu.VMEM((half_n - 1, r, c4), BF16),
            pltpu.VMEM((SECTORS, r, c4), BF16),
        ]
    vmem = pl.BlockSpec(memory_space=pltpu.VMEM)
    hbm = pl.BlockSpec(memory_space=pl.ANY)
    results = pl.pallas_call(
        functools.partial(kernel, lat_n, scale),
        out_shape=out_shape,
        in_specs=[vmem] * 2 + [hbm] * 5,
        out_specs=(hbm,) * 6,
        scratch_shapes=scratch,
        compiler_params=pltpu.CompilerParams(
            collective_id=0, has_side_effects=True, vmem_limit_bytes=56 * 1024 * 1024
        ),
    )(tokens, ocean_count, cotangent, w_qkv, w_out, w_up, w_down)
    return pl.pallas_call(
        hand_over,
        out_shape=out_shape,
        in_specs=[pl.BlockSpec(memory_space=pltpu.HBM)] * 6,
        out_specs=(hbm,) * 6,
        scratch_shapes=[pltpu.SemaphoreType.DMA((6,))],
    )(*results)


def solution(mesh):
    rows = P("lat", "lon", None)
    in_specs = (rows, P("lat", "lon"), P(), P(), P(), P(), rows)
    out_specs = (rows, rows, P("lat", None), P("lat", None), P("lat", None), P("lat", None))
    return jax.shard_map(
        functools.partial(local, mesh.shape["lat"]),
        mesh=mesh,
        in_specs=in_specs,
        out_specs=out_specs,
        check_vma=False,
    )
```

```python
import functools
import math

import jax
import jax.numpy as jnp
from jax import lax
from jax.experimental import pallas as pl
from jax.experimental.pallas import tpu as pltpu
from jax.sharding import PartitionSpec as P

HEAD_DIM = 64
SECTORS = 4
QUAD = 4 * HEAD_DIM
LANES = 128
MESH = pl.DeviceIdType.MESH
F32 = jnp.float32
BF16 = jnp.bfloat16


def nn(a, b):
    return jnp.dot(a, b, preferred_element_type=F32)


def nt(a, b):
    return lax.dot_general(a, b, (((1,), (1,)), ((), ())), preferred_element_type=F32)


def tn(a, b):
    return lax.dot_general(a, b, (((0,), (0,)), ((), ())), preferred_element_type=F32)


def split_two(values):
    high = values.astype(BF16)
    return high, (values - high.astype(F32)).astype(BF16)


def norm_stats(values):
    average = jnp.mean(values, axis=-1, keepdims=True)
    centered = values - average
    variance = jnp.mean(centered * centered, axis=-1, keepdims=True)
    inverse = lax.rsqrt(variance + 1e-05)
    return centered * inverse, inverse


def norm_back(grad, normed, inverse):
    first = jnp.mean(grad, axis=-1, keepdims=True)
    second = jnp.mean(grad * normed, axis=-1, keepdims=True)
    return inverse * (grad - first - normed * second)


def head_mean(values, blocks):
    parts = []
    for start in range(0, values.shape[1], QUAD):
        high, low = split_two(values[:, start : start + QUAD])
        parts.append(nn(high, blocks) + nn(low, blocks))
    return jnp.concatenate(parts, axis=1)


def kernel(lat_n, scale, *refs):
    x_ref, count_ref, cot_hbm, wqkv_hbm, wout_hbm, wup_hbm, wdown_hbm = refs[:7]
    bo_hbm, gt_hbm, gqkv_hbm, gout_hbm, gup_hbm, gdown_hbm = refs[7:13]
    cot_ref, wqkv, wout, wup, wdown = refs[13:18]
    bo_ref, gt_ref, gqkv, gout, gup, gdown = refs[18:24]
    xg, cg, ka, va, ma, qa, probs, att_ref, ivb_ref, dq_ref, dk_ref, dv_ref, gaall, stats = refs[24:38]
    sem_s, sem_r, lat_s, lat_r, all_s, all_r, in_sem, out_sem = refs[38:46]
    bufs = refs[46:]
    rows, length, width = x_ref.shape
    count = rows * length
    quads = width // QUAD
    half_n = lat_n // 2

    lat = lax.axis_index("lat")
    lon = lax.axis_index("lon")
    x_pos, core = lon // 2, lon % 2
    hi, lo = lat // 2, lat % 2
    core_peer = (lat, x_pos * 2 + (1 - core))
    x_peer = (lat, (1 - x_pos) * 2 + core)
    far_peer = (lat, (1 - x_pos) * 2 + (1 - core))
    lo_peer = (hi * 2 + (1 - lo), lon)

    barrier = pltpu.get_barrier_semaphore()
    for peer in (core_peer, x_peer, far_peer, lo_peer):
        pl.semaphore_signal(barrier, inc=1, device_id=peer, device_id_type=MESH)

    def hi_peer(offset):
        return lax.rem(hi + offset, half_n)

    @pl.loop(1, half_n)
    def _(offset):
        pl.semaphore_signal(
            barrier, inc=1, device_id=(hi_peer(offset) * 2 + lo, lon), device_id_type=MESH
        )

    loads = []
    for i, (src, dst) in enumerate(
        ((wqkv_hbm, wqkv), (wout_hbm, wout), (cot_hbm, cot_ref), (wup_hbm, wup), (wdown_hbm, wdown))
    ):
        load = pltpu.make_async_copy(src, dst, in_sem.at[i])
        load.start()
        loads.append(load)

    cg[0] = jnp.zeros_like(cg[0])
    counts = count_ref[...]
    for r in range(rows):
        cg[0, r : r + 1] = jnp.broadcast_to(counts[:, r : r + 1], (1, LANES))
    pl.semaphore_wait(barrier, 4 + half_n - 1)

    def remote(src, dst, send, recv, peer):
        return pltpu.make_async_remote_copy(
            src_ref=src, dst_ref=dst, send_sem=send, recv_sem=recv,
            device_id=peer, device_id_type=MESH,
        )

    def gather(src, buf, base):
        near = remote(src, buf.at[1], sem_s.at[base], sem_r.at[base], core_peer)
        across = remote(src, buf.at[2], sem_s.at[base + 1], sem_r.at[base + 1], x_peer)
        onward = remote(buf.at[2], buf.at[3], sem_s.at[base + 2], sem_r.at[base + 2], core_peer)
        across.start()
        near.start()
        return near, across, onward

    c_near, c_across, c_onward = gather(cg.at[0], cg, 9)
    x_near, x_across, x_onward = gather(x_ref, xg, 0)

    lane = lax.broadcasted_iota(jnp.int32, (1, QUAD), 1) // HEAD_DIM
    lane_f = [jnp.where(lane == h, 1.0, 0.0).astype(F32) for h in range(4)]
    lane_b = [m.astype(BF16) for m in lane_f]
    blocks = jnp.where(
        lax.broadcasted_iota(jnp.int32, (QUAD, QUAD), 0) // HEAD_DIM
        == lax.broadcasted_iota(jnp.int32, (QUAD, QUAD), 1) // HEAD_DIM,
        1.0 / HEAD_DIM,
        0.0,
    ).astype(BF16)
    heads = width // HEAD_DIM
    head_row = lax.broadcasted_iota(jnp.int32, (heads, width), 0)
    head_col = lax.broadcasted_iota(jnp.int32, (heads, width), 1)
    pick_sum = jnp.where(head_col // HEAD_DIM == head_row, 1.0, 0.0).astype(BF16)
    pick_one = jnp.where(head_col == head_row * HEAD_DIM, 1.0, 0.0).astype(BF16)
    place = lax.broadcasted_iota(jnp.int32, (length, LANES), 0)

    def stack(tile):
        return jnp.concatenate([tile * lane_b[h] for h in range(4)], axis=0)

    def combine(tile):
        total = tile[:HEAD_DIM] * lane_f[0]
        for h in range(1, 4):
            total = total + tile[h * length : (h + 1) * length] * lane_f[h]
        return total

    def per_row(values):
        return values.reshape(rows, length, values.shape[-1])

    def unit(raw):
        parts = []
        for start in range(0, width, QUAD):
            piece = raw[:, start : start + QUAD]
            parts.append(nn((piece * piece).astype(BF16), blocks))
        return lax.rsqrt(jnp.concatenate(parts, axis=1) + 1e-06)

    def project_q(slot, normed_b):
        query_raw = nn(normed_b, wqkv[:, :width])
        q_inv = unit(query_raw)
        qa[:, pl.ds(slot * length, length), :] = per_row((query_raw * q_inv).astype(BF16))
        return query_raw, q_inv

    def project_kv(slot):
        block = (x_ref[...] if slot == 0 else xg[slot]).reshape(count, width)
        mask = jnp.concatenate(
            [jnp.where(place < cg[slot, r : r + 1, :], 1.0, 0.0) for r in range(rows)], axis=0
        )
        mask_wide = jnp.concatenate([mask] * (width // LANES), axis=1)
        normed, inverse = norm_stats(block.astype(F32))
        normed_b = normed.astype(BF16)
        if slot == 0:
            loads[0].wait()
        key_raw = nn(normed_b, wqkv[:, width : 2 * width])
        value = nn(normed_b, wqkv[:, 2 * width :])
        k_inv = unit(key_raw)
        at = pl.ds(slot * length, length)
        ka[:, at, :] = per_row((key_raw * k_inv * mask_wide).astype(BF16))
        va[:, at, :] = per_row((value * mask_wide).astype(BF16))
        ma[:, at, :] = per_row(mask.astype(BF16))
        return normed, inverse, normed_b, key_raw, k_inv, mask_wide

    normed, inverse, normed_b, key_raw, k_inv, mask_wide = project_kv(0)
    query_raw, q_inv = project_q(0, normed_b)
    c_across.wait_recv()
    c_onward.start()
    c_near.wait_recv()
    x_near.wait_recv()
    normed_near = project_kv(1)[2]
    x_across.wait_recv()
    x_onward.start()
    normed_across = project_kv(2)[2]
    c_onward.wait_recv()
    x_onward.wait_recv()
    normed_far = project_kv(3)[2]

    logit = 8.0 / HEAD_DIM

    for r in range(rows):
        for qd in range(quads):
            cs = slice(qd * QUAD, (qd + 1) * QUAD)
            key, value = ka[r, :, cs], va[r, :, cs]
            score = jnp.exp(nt(stack(qa[r, 0:length, cs]), key) * logit - 8.0)
            score_b = score.astype(BF16)
            part = 1.0 / nn(score_b, ma[r])
            part = jnp.concatenate([part, part], axis=1)
            probs[r, qd] = score * part
            att_ref[r, :, cs] = combine(nn(score_b, value) * part)
            ivb_ref[r, :, cs] = combine(part)

    pending = {}

    def order(c):
        near = (x_pos, lo, x_peer, lo_peer) if c == 5 else (lo, x_pos, lo_peer, x_peer)
        return near

    def chunk(c):
        return bufs[9 * c : 9 * c + 9]

    def begin(c, left, right):
        part, from_core = chunk(c)[:2]
        n, r, c4 = part.shape[-3:]
        full = tn(left, right) * scale
        for l in range(SECTORS):
            piece = full[:, l * c4 : (l + 1) * c4].reshape(n, 2, r, c4).astype(BF16)
            for low in range(2):
                where = (l // 2, low) if c == 5 else (low, l // 2)
                part[(l % 2,) + where] = piece[:, low]
        at = 12 + 3 * c
        copy = remote(part.at[1 - core], from_core, sem_s.at[at], sem_r.at[at], core_peer)
        copy.start()
        pending[c] = copy

    def add(*terms):
        total = terms[0].astype(F32)
        for term in terms[1:]:
            total = total + term.astype(F32)
        return total.astype(BF16)

    def second(c):
        part, from_core, to_one, from_one = chunk(c)[:4]
        first_pos, _, first_peer, _ = order(c)
        pending[c].wait()
        to_one[...] = add(part[core, 1 - first_pos], from_core[1 - first_pos])
        at = 12 + 3 * c + 1
        copy = remote(to_one, from_one, sem_s.at[at], sem_r.at[at], first_peer)
        copy.start()
        pending[c] = copy

    def third(c):
        part, from_core, _, from_one, to_two, from_two = chunk(c)[:6]
        one, two, _, peer = order(c)
        pending[c].wait()
        to_two[...] = add(part[core, one, 1 - two], from_core[one, 1 - two], from_one[1 - two])
        at = 12 + 3 * c + 2
        copy = remote(to_two, from_two, sem_s.at[at], sem_r.at[at], peer)
        copy.start()
        pending[c] = copy

    def lat_copy(c, offset):
        total, from_lat = chunk(c)[6:8]
        target = hi_peer(offset)
        return remote(
            total.at[target], from_lat.at[offset - 1],
            lat_s.at[c, offset - 1], lat_r.at[c, offset - 1], (target * 2 + lo, lon),
        )

    def fourth(c):
        part, from_core, _, from_one, _, from_two, total, _, _ = chunk(c)
        one, two, _, _ = order(c)
        pending[c].wait()
        total[...] = add(part[core, one, two], from_core[one, two], from_one[two], from_two[...])

        @pl.loop(1, half_n)
        def _(offset):
            lat_copy(c, offset).start()

    def fifth(c):
        total, from_lat, everyone = chunk(c)[6:9]

        @pl.loop(1, half_n)
        def _(offset):
            lat_copy(c, offset).wait()

        everyone[lon] = (
            total[hi].astype(F32) + jnp.sum(from_lat[...].astype(F32), axis=0)
        ).astype(BF16)
        copies = []
        for i, peer in enumerate((x_peer, far_peer, core_peer)):
            copy = remote(
                everyone.at[lon], everyone.at[lon], all_s.at[c, i], all_r.at[c, i], peer
            )
            copy.start()
            copies.append(copy)
        pending[c] = copies

    stores = []

    def store(src, dst):
        copy = pltpu.make_async_copy(src, dst, out_sem.at[len(stores)])
        copy.start()
        stores.append(copy)

    def finish(c, out, first):
        everyone = chunk(c)[8]
        c4 = everyone.shape[-1]
        for copy in pending[c]:
            copy.wait()
        for l in range(SECTORS):
            out[:, first + l * c4 : first + (l + 1) * c4] = everyone[l].astype(F32)

    for load in loads[1:]:
        load.wait()
    tokens = x_ref[...].reshape(count, width).astype(F32)
    cotangent = cot_ref[...].reshape(count, width).astype(F32)
    grad_branch = (mask_wide * cotangent).astype(BF16)
    attended = att_ref[...].reshape(count, width)
    attended_b = attended.astype(BF16)
    middle = tokens + mask_wide * nn(attended_b, wout[...])
    normed_two, inverse_two = norm_stats(middle)
    normed_two_b = normed_two.astype(BF16)
    lifted = nn(normed_two_b, wup[...])
    root = math.sqrt(2.0 / math.pi)
    square = lifted * lifted
    curve = jnp.tanh(root * lifted * (1.0 + 0.044715 * square))
    half = 0.5 * (1.0 + curve)
    active = (lifted * half).astype(BF16)
    slope = half + 0.5 * lifted * (1.0 - curve * curve) * (root * (1.0 + 3 * 0.044715 * square))
    begin(0, active, grad_branch)

    grad_lifted = (slope * nt(grad_branch, wdown[...])).astype(BF16)
    grad_middle = cotangent + norm_back(nt(grad_lifted, wup[...]), normed_two, inverse_two)
    second(0)
    grad_attn = (mask_wide * grad_middle).astype(BF16)
    grad_attended = nt(grad_attn, wout[...]).astype(BF16)
    gaall[0] = per_row(grad_attended)
    g_near, g_across, g_onward = gather(gaall.at[0], gaall, 3)
    product = per_row(grad_attended.astype(F32) * attended)
    for r in range(rows):
        high, low = split_two(ivb_ref[r])
        part = nt(pick_one, high) + nt(pick_one, low)
        high, low = split_two(product[r])
        delta = nt(pick_sum, high) + nt(pick_sum, low)
        pair = jnp.concatenate([part, delta], axis=0)
        stats[0, r] = jnp.concatenate([pair, jnp.zeros_like(pair)], axis=1)
    s_near, s_across, s_onward = gather(stats.at[0], stats, 6)

    begin(1, normed_two_b, grad_lifted)
    begin(2, attended_b, grad_attn)
    second(1)
    second(2)
    bo_ref[...] = per_row((middle + mask_wide * nn(active, wdown[...])).astype(BF16))
    store(bo_ref, bo_hbm)
    project_q(1, normed_near)
    project_q(2, normed_across)
    project_q(3, normed_far)
    third(0)
    g_across.wait_recv()
    g_onward.start()
    s_across.wait_recv()
    s_onward.start()

    for r in range(rows):
        for qd in range(quads):
            cs = slice(qd * QUAD, (qd + 1) * QUAD)
            key, value = ka[r, :, cs], va[r, :, cs]
            tall = stack(gaall[0, r, :, cs])
            delta = jnp.sum(
                tall.astype(F32) * jnp.concatenate([att_ref[r, :, cs]] * 4, axis=0),
                axis=-1,
                keepdims=True,
            )
            back = (probs[r, qd] * (nt(tall, value) - delta) * logit).astype(BF16)
            dq_ref[r, :, cs] = combine(nn(back, key))

    def head_back(grad, raw, inv):
        return inv * (grad - raw * (inv * inv) * head_mean(raw * grad, blocks))

    grad_q = head_back(dq_ref[...].reshape(count, width), query_raw, q_inv).astype(BF16)
    begin(3, normed_b, grad_q)
    for copy in (g_near, s_near, g_onward, s_onward):
        copy.wait_recv()
    second(3)
    third(1)

    for r in range(rows):
        stat = jnp.concatenate([stats[s, r][:, :length] for s in range(SECTORS)], axis=1)
        for qd in range(quads):
            cs = slice(qd * QUAD, (qd + 1) * QUAD)
            query = qa[r, :, cs]
            grad = jnp.concatenate([gaall[s, r, :, cs] for s in range(SECTORS)], axis=0)

            def spread(base):
                return jnp.concatenate(
                    [
                        jnp.broadcast_to(stat[base + h : base + h + 1], (length, QUAD))
                        for h in range(qd * 4, qd * 4 + 4)
                    ],
                    axis=0,
                )

            score = jnp.exp(nt(stack(ka[r, 0:length, cs]), query) * logit - 8.0) * spread(0)
            deep = nt(stack(va[r, 0:length, cs]), grad)
            back = (score * (deep - spread(heads)) * logit).astype(BF16)
            dk_ref[r, :, cs] = combine(nn(back, query))
            dv_ref[r, :, cs] = combine(nn(score.astype(BF16), grad))

    grad_v = (dv_ref[...].reshape(count, width) * mask_wide).astype(BF16)
    begin(4, normed_b, grad_v)
    third(2)
    fourth(0)
    grad_k = head_back(
        dk_ref[...].reshape(count, width) * mask_wide, key_raw, k_inv
    ).astype(BF16)
    begin(5, normed_b, grad_k)
    second(4)
    second(5)
    third(3)
    fourth(1)
    fourth(2)
    fifth(0)
    grad_normed = (
        nt(grad_q, wqkv[:, :width])
        + nt(grad_k, wqkv[:, width : 2 * width])
        + nt(grad_v, wqkv[:, 2 * width :])
    )
    gt_ref[...] = per_row((grad_middle + norm_back(grad_normed, normed, inverse)).astype(BF16))
    store(gt_ref, gt_hbm)
    third(4)
    fourth(3)
    third(5)
    fifth(1)
    finish(0, gdown, 0)
    store(gdown, gdown_hbm)
    fourth(4)
    fifth(2)
    fourth(5)
    finish(1, gup, 0)
    store(gup, gup_hbm)
    fifth(3)
    fifth(4)
    finish(2, gout, 0)
    store(gout, gout_hbm)
    finish(3, gqkv, 0)
    for group in (
        (g_near, g_across, g_onward), (s_near, s_across, s_onward),
        (x_near, x_across, x_onward), (c_near, c_across, c_onward),
    ):
        for copy in group:
            copy.wait_send()
    fifth(5)
    finish(4, gqkv, 2 * width)
    finish(5, gqkv, width)
    store(gqkv, gqkv_hbm)
    for copy in stores:
        copy.wait()


def hand_over(*refs):
    sems = refs[12]
    copies = [pltpu.make_async_copy(refs[i], refs[6 + i], sems.at[i]) for i in range(6)]
    for copy in copies:
        copy.start()
    for copy in copies:
        copy.wait()


def local(lat_n, tokens, ocean_count, w_qkv, w_out, w_up, w_down, cotangent):
    rows, length, width = tokens.shape
    heads = width // HEAD_DIM
    hidden = w_up.shape[1]
    half_n = lat_n // 2
    scale = 1.0 / math.sqrt(rows * lat_n * length * SECTORS)
    quads = width // QUAD
    full = length * SECTORS
    out_shape = (
        jax.ShapeDtypeStruct(tokens.shape, BF16),
        jax.ShapeDtypeStruct(tokens.shape, BF16),
        jax.ShapeDtypeStruct((width // lat_n, 3 * width), F32),
        jax.ShapeDtypeStruct((width // lat_n, width), F32),
        jax.ShapeDtypeStruct((width // lat_n, hidden), F32),
        jax.ShapeDtypeStruct((hidden // lat_n, width), F32),
    )
    scratch = [pltpu.VMEM(a.shape, BF16) for a in (cotangent, w_qkv, w_out, w_up, w_down)]
    scratch += [pltpu.VMEM(a.shape, a.dtype) for a in out_shape]
    scratch += [
        pltpu.VMEM((SECTORS, rows, length, width), BF16),
        pltpu.VMEM((SECTORS, -(-rows // 8) * 8, LANES), jnp.int32),
        pltpu.VMEM((rows, full, width), BF16),
        pltpu.VMEM((rows, full, width), BF16),
        pltpu.VMEM((rows, full, LANES), BF16),
        pltpu.VMEM((rows, full, width), BF16),
        pltpu.VMEM((rows, quads, 4 * length, full), F32),
        pltpu.VMEM((rows, length, width), F32),
        pltpu.VMEM((rows, length, width), F32),
        pltpu.VMEM((rows, length, width), F32),
        pltpu.VMEM((rows, length, width), F32),
        pltpu.VMEM((rows, length, width), F32),
        pltpu.VMEM((SECTORS, rows, length, width), BF16),
        pltpu.VMEM((SECTORS, rows, 2 * heads, LANES), F32),
        pltpu.SemaphoreType.DMA((30,)),
        pltpu.SemaphoreType.DMA((30,)),
        pltpu.SemaphoreType.DMA((6, half_n - 1)),
        pltpu.SemaphoreType.DMA((6, half_n - 1)),
        pltpu.SemaphoreType.DMA((6, 3)),
        pltpu.SemaphoreType.DMA((6, 3)),
        pltpu.SemaphoreType.DMA((5,)),
        pltpu.SemaphoreType.DMA((6,)),
    ]
    for tall, broad in ((hidden, width), (width, hidden)) + ((width, width),) * 4:
        r, c4 = tall // lat_n, broad // SECTORS
        scratch += [
            pltpu.VMEM((2, 2, 2, half_n, r, c4), BF16),
            pltpu.VMEM((2, 2, half_n, r, c4), BF16),
            pltpu.VMEM((2, half_n, r, c4), BF16),
            pltpu.VMEM((2, half_n, r, c4), BF16),
            pltpu.VMEM((half_n, r, c4), BF16),
            pltpu.VMEM((half_n, r, c4), BF16),
            pltpu.VMEM((half_n, r, c4), BF16),
            pltpu.VMEM((half_n - 1, r, c4), BF16),
            pltpu.VMEM((SECTORS, r, c4), BF16),
        ]
    vmem = pl.BlockSpec(memory_space=pltpu.VMEM)
    hbm = pl.BlockSpec(memory_space=pl.ANY)
    results = pl.pallas_call(
        functools.partial(kernel, lat_n, scale),
        out_shape=out_shape,
        in_specs=[vmem] * 2 + [hbm] * 5,
        out_specs=(hbm,) * 6,
        scratch_shapes=scratch,
        compiler_params=pltpu.CompilerParams(
            collective_id=0, has_side_effects=True, vmem_limit_bytes=56 * 1024 * 1024
        ),
    )(tokens, ocean_count.T, cotangent, w_qkv, w_out, w_up, w_down)
    return pl.pallas_call(
        hand_over,
        out_shape=out_shape,
        in_specs=[vmem] * 6,
        out_specs=(hbm,) * 6,
        scratch_shapes=[pltpu.SemaphoreType.DMA((6,))],
    )(*results)


def solution(mesh):
    rows = P("lat", "lon", None)
    in_specs = (rows, P("lat", "lon"), P(), P(), P(), P(), rows)
    out_specs = (rows, rows, P("lat", None), P("lat", None), P("lat", None), P("lat", None))
    return jax.shard_map(
        functools.partial(local, mesh.shape["lat"]),
        mesh=mesh,
        in_specs=in_specs,
        out_specs=out_specs,
        check_vma=False,
    )
```

```python
import functools
import math

import jax
import jax.numpy as jnp
from jax import lax
from jax.experimental import pallas as pl
from jax.experimental.pallas import tpu as pltpu
from jax.sharding import PartitionSpec as P

HEAD_DIM = 64
SECTORS = 4
QUAD = 4 * HEAD_DIM
LANES = 128
MESH = pl.DeviceIdType.MESH
F32 = jnp.float32
BF16 = jnp.bfloat16


def nn(a, b):
    return jnp.dot(a, b, preferred_element_type=F32)


def nt(a, b):
    return lax.dot_general(a, b, (((1,), (1,)), ((), ())), preferred_element_type=F32)


def tn(a, b):
    return lax.dot_general(a, b, (((0,), (0,)), ((), ())), preferred_element_type=F32)


def split_two(values):
    high = values.astype(BF16)
    return high, (values - high.astype(F32)).astype(BF16)


def norm_stats(values):
    average = jnp.mean(values, axis=-1, keepdims=True)
    centered = values - average
    variance = jnp.mean(centered * centered, axis=-1, keepdims=True)
    inverse = lax.rsqrt(variance + 1e-05)
    return centered * inverse, inverse


def norm_back(grad, normed, inverse):
    first = jnp.mean(grad, axis=-1, keepdims=True)
    second = jnp.mean(grad * normed, axis=-1, keepdims=True)
    return inverse * (grad - first - normed * second)


def head_mean(values, blocks):
    parts = []
    for start in range(0, values.shape[1], QUAD):
        high, low = split_two(values[:, start : start + QUAD])
        parts.append(nn(high, blocks) + nn(low, blocks))
    return jnp.concatenate(parts, axis=1)


def kernel(lat_n, scale, *refs):
    x_ref, count_ref, cot_hbm, wqkv_hbm, wout_hbm, wup_hbm, wdown_hbm = refs[:7]
    bo_hbm, gt_hbm, gqkv_hbm, gout_hbm, gup_hbm, gdown_hbm = refs[7:13]
    cot_ref, wqkv, wout, wup, wdown = refs[13:18]
    bo_ref, gt_ref, gqkv, gout, gup, gdown = refs[18:24]
    xg, cg, ka, va, ma, qa, probs, att_ref, ivb_ref, dq_ref, dk_ref, dv_ref, gaall, stats = refs[24:38]
    sem_s, sem_r, lat_s, lat_r, all_s, all_r, in_sem, out_sem = refs[38:46]
    bufs = refs[46:]
    rows, length, width = x_ref.shape
    count = rows * length
    quads = width // QUAD
    half_n = lat_n // 2

    lat = lax.axis_index("lat")
    lon = lax.axis_index("lon")
    x_pos, core = lon // 2, lon % 2
    hi, lo = lat // 2, lat % 2
    core_peer = (lat, x_pos * 2 + (1 - core))
    x_peer = (lat, (1 - x_pos) * 2 + core)
    far_peer = (lat, (1 - x_pos) * 2 + (1 - core))
    lo_peer = (hi * 2 + (1 - lo), lon)

    barrier = pltpu.get_barrier_semaphore()
    for peer in (core_peer, x_peer, far_peer, lo_peer):
        pl.semaphore_signal(barrier, inc=1, device_id=peer, device_id_type=MESH)

    def hi_peer(offset):
        return lax.rem(hi + offset, half_n)

    @pl.loop(1, half_n)
    def _(offset):
        pl.semaphore_signal(
            barrier, inc=1, device_id=(hi_peer(offset) * 2 + lo, lon), device_id_type=MESH
        )

    loads = []
    for i, (src, dst) in enumerate(
        ((wqkv_hbm, wqkv), (wout_hbm, wout), (cot_hbm, cot_ref), (wup_hbm, wup), (wdown_hbm, wdown))
    ):
        load = pltpu.make_async_copy(src, dst, in_sem.at[i])
        load.start()
        loads.append(load)

    cg[0] = jnp.zeros_like(cg[0])
    counts = count_ref[...]
    for r in range(rows):
        cg[0, r : r + 1] = jnp.broadcast_to(counts[:, r : r + 1], (1, LANES))
    normed, inverse = norm_stats(x_ref[...].reshape(count, width).astype(F32))
    normed_b = normed.astype(BF16)
    pl.semaphore_wait(barrier, 4 + half_n - 1)

    def remote(src, dst, send, recv, peer):
        return pltpu.make_async_remote_copy(
            src_ref=src, dst_ref=dst, send_sem=send, recv_sem=recv,
            device_id=peer, device_id_type=MESH,
        )

    def gather(src, buf, base):
        near = remote(src, buf.at[1], sem_s.at[base], sem_r.at[base], core_peer)
        across = remote(src, buf.at[2], sem_s.at[base + 1], sem_r.at[base + 1], x_peer)
        onward = remote(buf.at[2], buf.at[3], sem_s.at[base + 2], sem_r.at[base + 2], core_peer)
        across.start()
        near.start()
        return near, across, onward

    c_near, c_across, c_onward = gather(cg.at[0], cg, 9)
    x_near = remote(x_ref, xg.at[1], sem_s.at[0], sem_r.at[0], core_peer)
    x_across, x_onward = [], []
    for r in range(rows):
        at = 30 + 2 * r
        x_across.append(
            remote(x_ref.at[r], xg.at[2, r], sem_s.at[at], sem_r.at[at], x_peer)
        )
        x_onward.append(
            remote(xg.at[2, r], xg.at[3, r], sem_s.at[at + 1], sem_r.at[at + 1], core_peer)
        )
        x_across[r].start()
        if r == 0:
            x_near.start()

    lane = lax.broadcasted_iota(jnp.int32, (1, QUAD), 1) // HEAD_DIM
    lane_f = [jnp.where(lane == h, 1.0, 0.0).astype(F32) for h in range(4)]
    lane_b = [m.astype(BF16) for m in lane_f]
    blocks = jnp.where(
        lax.broadcasted_iota(jnp.int32, (QUAD, QUAD), 0) // HEAD_DIM
        == lax.broadcasted_iota(jnp.int32, (QUAD, QUAD), 1) // HEAD_DIM,
        1.0 / HEAD_DIM,
        0.0,
    ).astype(BF16)
    heads = width // HEAD_DIM
    head_row = lax.broadcasted_iota(jnp.int32, (heads, width), 0)
    head_col = lax.broadcasted_iota(jnp.int32, (heads, width), 1)
    pick_sum = jnp.where(head_col // HEAD_DIM == head_row, 1.0, 0.0).astype(BF16)
    pick_one = jnp.where(head_col == head_row * HEAD_DIM, 1.0, 0.0).astype(BF16)
    place = lax.broadcasted_iota(jnp.int32, (length, LANES), 0)

    def stack(tile):
        return jnp.concatenate([tile * lane_b[h] for h in range(4)], axis=0)

    def combine(tile):
        total = tile[:HEAD_DIM] * lane_f[0]
        for h in range(1, 4):
            total = total + tile[h * length : (h + 1) * length] * lane_f[h]
        return total

    def per_row(values):
        return values.reshape(rows, length, values.shape[-1])

    def unit(raw):
        parts = []
        for start in range(0, width, QUAD):
            piece = raw[:, start : start + QUAD]
            parts.append(nn((piece * piece).astype(BF16), blocks))
        return lax.rsqrt(jnp.concatenate(parts, axis=1) + 1e-06)

    def query_of(normed_b):
        query_raw = nn(normed_b, wqkv[:, :width])
        q_inv = unit(query_raw)
        return (query_raw * q_inv).astype(BF16), query_raw, q_inv

    def mask_of(slot, r):
        return jnp.where(place < cg[slot, r : r + 1, :], 1.0, 0.0)

    def kv_of(normed_b, mask):
        mask_wide = jnp.concatenate([mask] * (width // LANES), axis=1)
        key_raw = nn(normed_b, wqkv[:, width : 2 * width])
        value = nn(normed_b, wqkv[:, 2 * width :])
        k_inv = unit(key_raw)
        key = (key_raw * k_inv * mask_wide).astype(BF16)
        return key, (value * mask_wide).astype(BF16), key_raw, k_inv, mask_wide

    mask = jnp.concatenate([mask_of(0, r) for r in range(rows)], axis=0)
    loads[0].wait()
    key, value, key_raw, k_inv, mask_wide = kv_of(normed_b, mask)
    ka[:, 0:length, :], va[:, 0:length, :] = per_row(key), per_row(value)
    ma[:, 0:length, :] = per_row(mask.astype(BF16))
    query, query_raw, q_inv = query_of(normed_b)
    qa[:, 0:length, :] = per_row(query)
    normed_t = normed_b.T

    c_across.wait_recv()
    c_onward.start()
    c_near.wait_recv()
    x_near.wait_recv()
    normed_near = norm_stats(xg[1].reshape(count, width).astype(F32))[0].astype(BF16)
    mask = jnp.concatenate([mask_of(1, r) for r in range(rows)], axis=0)
    key, value = kv_of(normed_near, mask)[:2]
    at = slice(length, 2 * length)
    ka[:, at, :], va[:, at, :] = per_row(key), per_row(value)
    ma[:, at, :] = per_row(mask.astype(BF16))

    logit = 8.0 / HEAD_DIM
    normed_far = []
    x_across[0].wait_recv()
    x_onward[0].start()
    c_onward.wait_recv()
    for r in range(rows):
        x_onward[r].wait_recv()
        if r + 1 < rows:
            x_across[r + 1].wait_recv()
            x_onward[r + 1].start()
        block = jnp.concatenate([xg[2, r], xg[3, r]], axis=0).astype(F32)
        normed_far.append(norm_stats(block)[0].astype(BF16))
        mask = jnp.concatenate([mask_of(2, r), mask_of(3, r)], axis=0)
        far_key, far_value = kv_of(normed_far[r], mask)[:2]
        at = slice(2 * length, 4 * length)
        ka[r, at, :], va[r, at, :], ma[r, at, :] = far_key, far_value, mask.astype(BF16)
        for qd in range(quads):
            cs = slice(qd * QUAD, (qd + 1) * QUAD)
            key, value = ka[r, :, cs], va[r, :, cs]
            score = jnp.exp(nt(stack(qa[r, 0:length, cs]), key) * logit - 8.0)
            score_b = score.astype(BF16)
            part = 1.0 / nn(score_b, ma[r])
            part = jnp.concatenate([part, part], axis=1)
            probs[r, qd] = score * part
            att_ref[r, :, cs] = combine(nn(score_b, value) * part)
            ivb_ref[r, :, cs] = combine(part)

    pending = {}

    def order(c):
        near = (x_pos, lo, x_peer, lo_peer) if c == 5 else (lo, x_pos, lo_peer, x_peer)
        return near

    def chunk(c):
        return bufs[9 * c : 9 * c + 9]

    def begin(c, left, right):
        part, from_core = chunk(c)[:2]
        n, r, c4 = part.shape[-3:]
        full = nn(normed_t, right) if left is None else tn(left, right)
        for l in range(SECTORS):
            piece = full[:, l * c4 : (l + 1) * c4].reshape(n, 2, r, c4).astype(BF16)
            for low in range(2):
                where = (l // 2, low) if c == 5 else (low, l // 2)
                part[(l % 2,) + where] = piece[:, low]
        at = 12 + 3 * c
        copy = remote(part.at[1 - core], from_core, sem_s.at[at], sem_r.at[at], core_peer)
        copy.start()
        pending[c] = copy

    def add(*terms):
        total = terms[0].astype(F32)
        for term in terms[1:]:
            total = total + term.astype(F32)
        return total.astype(BF16)

    def second(c):
        part, from_core, to_one, from_one = chunk(c)[:4]
        first_pos, _, first_peer, _ = order(c)
        pending[c].wait()
        to_one[...] = add(part[core, 1 - first_pos], from_core[1 - first_pos])
        at = 12 + 3 * c + 1
        copy = remote(to_one, from_one, sem_s.at[at], sem_r.at[at], first_peer)
        copy.start()
        pending[c] = copy

    def third(c):
        part, from_core, _, from_one, to_two, from_two = chunk(c)[:6]
        one, two, _, peer = order(c)
        pending[c].wait()
        to_two[...] = add(part[core, one, 1 - two], from_core[one, 1 - two], from_one[1 - two])
        at = 12 + 3 * c + 2
        copy = remote(to_two, from_two, sem_s.at[at], sem_r.at[at], peer)
        copy.start()
        pending[c] = copy

    def lat_copy(c, offset):
        total, from_lat = chunk(c)[6:8]
        target = hi_peer(offset)
        return remote(
            total.at[target], from_lat.at[offset - 1],
            lat_s.at[c, offset - 1], lat_r.at[c, offset - 1], (target * 2 + lo, lon),
        )

    def fourth(c):
        part, from_core, _, from_one, _, from_two, total, _, _ = chunk(c)
        one, two, _, _ = order(c)
        pending[c].wait()
        total[...] = add(part[core, one, two], from_core[one, two], from_one[two], from_two[...])

        @pl.loop(1, half_n)
        def _(offset):
            lat_copy(c, offset).start()

    def fifth(c):
        total, from_lat, everyone = chunk(c)[6:9]

        @pl.loop(1, half_n)
        def _(offset):
            lat_copy(c, offset).wait()

        everyone[lon] = (
            total[hi].astype(F32) + jnp.sum(from_lat[...].astype(F32), axis=0)
        ).astype(BF16)
        copies = []
        for i, peer in enumerate((x_peer, far_peer, core_peer)):
            copy = remote(
                everyone.at[lon], everyone.at[lon], all_s.at[c, i], all_r.at[c, i], peer
            )
            copy.start()
            copies.append(copy)
        pending[c] = copies

    stores = []

    def store(src, dst):
        copy = pltpu.make_async_copy(src, dst, out_sem.at[len(stores)])
        copy.start()
        stores.append(copy)

    def finish(c, out, first):
        everyone = chunk(c)[8]
        c4 = everyone.shape[-1]
        for copy in pending[c]:
            copy.wait()
        for l in range(SECTORS):
            out[:, first + l * c4 : first + (l + 1) * c4] = everyone[l].astype(F32) * scale

    for load in loads[1:]:
        load.wait()
    tokens = x_ref[...].reshape(count, width).astype(F32)
    cotangent = cot_ref[...].reshape(count, width).astype(F32)
    grad_branch = (mask_wide * cotangent).astype(BF16)
    attended = att_ref[...].reshape(count, width)
    attended_b = attended.astype(BF16)
    middle = tokens + mask_wide * nn(attended_b, wout[...])
    normed_two, inverse_two = norm_stats(middle)
    normed_two_b = normed_two.astype(BF16)
    lifted = nn(normed_two_b, wup[...])
    root = math.sqrt(2.0 / math.pi)
    square = lifted * lifted
    curve = jnp.tanh(root * lifted * (1.0 + 0.044715 * square))
    half = 0.5 * (1.0 + curve)
    active = (lifted * half).astype(BF16)
    slope = half + 0.5 * lifted * (1.0 - curve * curve) * (root * (1.0 + 3 * 0.044715 * square))
    begin(0, active, grad_branch)

    grad_lifted = (slope * nt(grad_branch, wdown[...])).astype(BF16)
    grad_middle = cotangent + norm_back(nt(grad_lifted, wup[...]), normed_two, inverse_two)
    second(0)
    grad_attn = (mask_wide * grad_middle).astype(BF16)
    grad_attended = nt(grad_attn, wout[...]).astype(BF16)
    gaall[0] = per_row(grad_attended)
    g_near, g_across, g_onward = gather(gaall.at[0], gaall, 3)
    product = per_row(grad_attended.astype(F32) * attended)
    for r in range(rows):
        high, low = split_two(ivb_ref[r])
        part = nt(pick_one, high) + nt(pick_one, low)
        high, low = split_two(product[r])
        delta = nt(pick_sum, high) + nt(pick_sum, low)
        pair = jnp.concatenate([part, delta], axis=0)
        stats[0, r] = jnp.concatenate([pair, jnp.zeros_like(pair)], axis=1)
    s_near, s_across, s_onward = gather(stats.at[0], stats, 6)

    begin(1, normed_two_b, grad_lifted)
    begin(2, attended_b, grad_attn)
    second(1)
    second(2)
    qa[:, length : 2 * length, :] = per_row(query_of(normed_near)[0])
    qa[:, 2 * length : 4 * length, :] = query_of(
        jnp.concatenate(normed_far, axis=0)
    )[0].reshape(rows, 2 * length, width)
    third(0)
    g_across.wait_recv()
    g_onward.start()
    s_across.wait_recv()
    s_onward.start()

    for r in range(rows):
        for qd in range(quads):
            cs = slice(qd * QUAD, (qd + 1) * QUAD)
            key, value = ka[r, :, cs], va[r, :, cs]
            tall = stack(gaall[0, r, :, cs])
            delta = jnp.sum(
                tall.astype(F32) * jnp.concatenate([att_ref[r, :, cs]] * 4, axis=0),
                axis=-1,
                keepdims=True,
            )
            back = (probs[r, qd] * (nt(tall, value) - delta) * logit).astype(BF16)
            dq_ref[r, :, cs] = combine(nn(back, key))

    def head_back(grad, raw, inv):
        return inv * (grad - raw * (inv * inv) * head_mean(raw * grad, blocks))

    grad_q = head_back(dq_ref[...].reshape(count, width), query_raw, q_inv).astype(BF16)
    begin(3, None, grad_q)
    for copy in (g_near, s_near, g_onward, s_onward):
        copy.wait_recv()
    second(3)
    third(1)

    for r in range(rows):
        stat = jnp.concatenate([stats[s, r][:, :length] for s in range(SECTORS)], axis=1)
        for qd in range(quads):
            cs = slice(qd * QUAD, (qd + 1) * QUAD)
            query = qa[r, :, cs]
            grad = jnp.concatenate([gaall[s, r, :, cs] for s in range(SECTORS)], axis=0)

            def spread(base):
                return jnp.concatenate(
                    [
                        jnp.broadcast_to(stat[base + h : base + h + 1], (length, QUAD))
                        for h in range(qd * 4, qd * 4 + 4)
                    ],
                    axis=0,
                )

            score = jnp.exp(nt(stack(ka[r, 0:length, cs]), query) * logit - 8.0) * spread(0)
            deep = nt(stack(va[r, 0:length, cs]), grad)
            back = (score * (deep - spread(heads)) * logit).astype(BF16)
            dk_ref[r, :, cs] = combine(nn(back, query))
            dv_ref[r, :, cs] = combine(nn(score.astype(BF16), grad))

    grad_v = (dv_ref[...].reshape(count, width) * mask_wide).astype(BF16)
    begin(4, None, grad_v)
    third(2)
    fourth(0)
    grad_k = head_back(
        dk_ref[...].reshape(count, width) * mask_wide, key_raw, k_inv
    ).astype(BF16)
    begin(5, None, grad_k)
    second(4)
    third(3)
    fourth(1)
    fourth(2)
    second(5)
    fifth(0)
    grad_normed = (
        nt(grad_q, wqkv[:, :width])
        + nt(grad_k, wqkv[:, width : 2 * width])
        + nt(grad_v, wqkv[:, 2 * width :])
    )
    gt_ref[...] = per_row((grad_middle + norm_back(grad_normed, normed, inverse)).astype(BF16))
    store(gt_ref, gt_hbm)
    third(4)
    fourth(3)
    bo_ref[...] = per_row((middle + mask_wide * nn(active, wdown[...])).astype(BF16))
    store(bo_ref, bo_hbm)
    third(5)
    fifth(1)
    finish(0, gdown, 0)
    store(gdown, gdown_hbm)
    fourth(4)
    fifth(2)
    fourth(5)
    finish(1, gup, 0)
    store(gup, gup_hbm)
    fifth(3)
    fifth(4)
    finish(2, gout, 0)
    store(gout, gout_hbm)
    finish(3, gqkv, 0)
    for group in (
        (g_near, g_across, g_onward), (s_near, s_across, s_onward),
        [x_near] + x_across + x_onward, (c_near, c_across, c_onward),
    ):
        for copy in group:
            copy.wait_send()
    fifth(5)
    finish(4, gqkv, 2 * width)
    finish(5, gqkv, width)
    store(gqkv, gqkv_hbm)
    for copy in stores:
        copy.wait()


def hand_over(*refs):
    sems = refs[12]
    copies = [pltpu.make_async_copy(refs[i], refs[6 + i], sems.at[i]) for i in range(6)]
    for copy in copies:
        copy.start()
    for copy in copies:
        copy.wait()


def local(lat_n, tokens, ocean_count, w_qkv, w_out, w_up, w_down, cotangent):
    rows, length, width = tokens.shape
    heads = width // HEAD_DIM
    hidden = w_up.shape[1]
    half_n = lat_n // 2
    scale = 1.0 / math.sqrt(rows * lat_n * length * SECTORS)
    quads = width // QUAD
    full = length * SECTORS
    out_shape = (
        jax.ShapeDtypeStruct(tokens.shape, BF16),
        jax.ShapeDtypeStruct(tokens.shape, BF16),
        jax.ShapeDtypeStruct((width // lat_n, 3 * width), F32),
        jax.ShapeDtypeStruct((width // lat_n, width), F32),
        jax.ShapeDtypeStruct((width // lat_n, hidden), F32),
        jax.ShapeDtypeStruct((hidden // lat_n, width), F32),
    )
    scratch = [pltpu.VMEM(a.shape, BF16) for a in (cotangent, w_qkv, w_out, w_up, w_down)]
    scratch += [pltpu.VMEM(a.shape, a.dtype) for a in out_shape]
    scratch += [
        pltpu.VMEM((SECTORS, rows, length, width), BF16),
        pltpu.VMEM((SECTORS, -(-rows // 8) * 8, LANES), jnp.int32),
        pltpu.VMEM((rows, full, width), BF16),
        pltpu.VMEM((rows, full, width), BF16),
        pltpu.VMEM((rows, full, LANES), BF16),
        pltpu.VMEM((rows, full, width), BF16),
        pltpu.VMEM((rows, quads, 4 * length, full), F32),
        pltpu.VMEM((rows, length, width), F32),
        pltpu.VMEM((rows, length, width), F32),
        pltpu.VMEM((rows, length, width), F32),
        pltpu.VMEM((rows, length, width), F32),
        pltpu.VMEM((rows, length, width), F32),
        pltpu.VMEM((SECTORS, rows, length, width), BF16),
        pltpu.VMEM((SECTORS, rows, 2 * heads, LANES), F32),
        pltpu.SemaphoreType.DMA((30 + 2 * rows,)),
        pltpu.SemaphoreType.DMA((30 + 2 * rows,)),
        pltpu.SemaphoreType.DMA((6, half_n - 1)),
        pltpu.SemaphoreType.DMA((6, half_n - 1)),
        pltpu.SemaphoreType.DMA((6, 3)),
        pltpu.SemaphoreType.DMA((6, 3)),
        pltpu.SemaphoreType.DMA((5,)),
        pltpu.SemaphoreType.DMA((6,)),
    ]
    for tall, broad in ((hidden, width), (width, hidden)) + ((width, width),) * 4:
        r, c4 = tall // lat_n, broad // SECTORS
        scratch += [
            pltpu.VMEM((2, 2, 2, half_n, r, c4), BF16),
            pltpu.VMEM((2, 2, half_n, r, c4), BF16),
            pltpu.VMEM((2, half_n, r, c4), BF16),
            pltpu.VMEM((2, half_n, r, c4), BF16),
            pltpu.VMEM((half_n, r, c4), BF16),
            pltpu.VMEM((half_n, r, c4), BF16),
            pltpu.VMEM((half_n, r, c4), BF16),
            pltpu.VMEM((half_n - 1, r, c4), BF16),
            pltpu.VMEM((SECTORS, r, c4), BF16),
        ]
    vmem = pl.BlockSpec(memory_space=pltpu.VMEM)
    hbm = pl.BlockSpec(memory_space=pl.ANY)
    results = pl.pallas_call(
        functools.partial(kernel, lat_n, scale),
        out_shape=out_shape,
        in_specs=[vmem] * 2 + [hbm] * 5,
        out_specs=(hbm,) * 6,
        scratch_shapes=scratch,
        compiler_params=pltpu.CompilerParams(
            collective_id=0, has_side_effects=True, vmem_limit_bytes=56 * 1024 * 1024
        ),
    )(tokens, ocean_count.T, cotangent, w_qkv, w_out, w_up, w_down)
    return pl.pallas_call(
        hand_over,
        out_shape=out_shape,
        in_specs=[vmem] * 6,
        out_specs=(hbm,) * 6,
        scratch_shapes=[pltpu.SemaphoreType.DMA((6,))],
    )(*results)


def solution(mesh):
    rows = P("lat", "lon", None)
    in_specs = (rows, P("lat", "lon"), P(), P(), P(), P(), rows)
    out_specs = (rows, rows, P("lat", None), P("lat", None), P("lat", None), P("lat", None))
    return jax.shard_map(
        functools.partial(local, mesh.shape["lat"]),
        mesh=mesh,
        in_specs=in_specs,
        out_specs=out_specs,
        check_vma=False,
    )
```

```python
import functools
import math

import jax
import jax.numpy as jnp
from jax import lax
from jax.experimental import pallas as pl
from jax.experimental.pallas import tpu as pltpu
from jax.sharding import PartitionSpec as P

HEAD_DIM = 64
SECTORS = 4
QUAD = 4 * HEAD_DIM
LANES = 128
MESH = pl.DeviceIdType.MESH
F32 = jnp.float32
BF16 = jnp.bfloat16


def nn(a, b):
    return jnp.dot(a, b, preferred_element_type=F32)


def nt(a, b):
    return lax.dot_general(a, b, (((1,), (1,)), ((), ())), preferred_element_type=F32)


def tn(a, b):
    return lax.dot_general(a, b, (((0,), (0,)), ((), ())), preferred_element_type=F32)


def split_two(values):
    high = values.astype(BF16)
    return high, (values - high.astype(F32)).astype(BF16)


def norm_stats(values):
    average = jnp.mean(values, axis=-1, keepdims=True)
    centered = values - average
    variance = jnp.mean(centered * centered, axis=-1, keepdims=True)
    inverse = lax.rsqrt(variance + 1e-05)
    return centered * inverse, inverse


def norm_back(grad, normed, inverse):
    first = jnp.mean(grad, axis=-1, keepdims=True)
    second = jnp.mean(grad * normed, axis=-1, keepdims=True)
    return inverse * (grad - first - normed * second)


def head_mean(values, blocks):
    parts = []
    for start in range(0, values.shape[1], QUAD):
        high, low = split_two(values[:, start : start + QUAD])
        parts.append(nn(high, blocks) + nn(low, blocks))
    return jnp.concatenate(parts, axis=1)


def kernel(lat_n, scale, *refs):
    x_ref, count_ref, cot_hbm, wqkv_hbm, wout_hbm, wup_hbm, wdown_hbm = refs[:7]
    bo_hbm, gt_hbm, gqkv_hbm, gout_hbm, gup_hbm, gdown_hbm = refs[7:13]
    cot_ref, wqkv, wout, wup, wdown = refs[13:18]
    bo_ref, gt_ref, gqkv, gout, gup, gdown = refs[18:24]
    xg, cg, ka, va, ma, qa, probs, att_ref, ivb_ref, dq_ref, dk_ref, dv_ref, gaall, stats, ntr = refs[24:39]
    sem_s, sem_r, lat_s, lat_r, all_s, all_r, in_sem, out_sem = refs[39:47]
    bufs = refs[47:]
    rows, length, width = x_ref.shape
    count = rows * length
    quads = width // QUAD
    half_n = lat_n // 2

    lat = lax.axis_index("lat")
    lon = lax.axis_index("lon")
    x_pos, core = lon // 2, lon % 2
    hi, lo = lat // 2, lat % 2
    core_peer = (lat, x_pos * 2 + (1 - core))
    x_peer = (lat, (1 - x_pos) * 2 + core)
    far_peer = (lat, (1 - x_pos) * 2 + (1 - core))
    lo_peer = (hi * 2 + (1 - lo), lon)

    barrier = pltpu.get_barrier_semaphore()
    for peer in (core_peer, x_peer, far_peer, lo_peer):
        pl.semaphore_signal(barrier, inc=1, device_id=peer, device_id_type=MESH)

    def hi_peer(offset):
        return lax.rem(hi + offset, half_n)

    @pl.loop(1, half_n)
    def _(offset):
        pl.semaphore_signal(
            barrier, inc=1, device_id=(hi_peer(offset) * 2 + lo, lon), device_id_type=MESH
        )

    loads = []
    for i, (src, dst) in enumerate(
        ((wqkv_hbm, wqkv), (wout_hbm, wout), (cot_hbm, cot_ref), (wup_hbm, wup), (wdown_hbm, wdown))
    ):
        load = pltpu.make_async_copy(src, dst, in_sem.at[i])
        load.start()
        loads.append(load)

    cg[0] = jnp.zeros_like(cg[0])
    counts = count_ref[...]
    for r in range(rows):
        cg[0, r : r + 1] = jnp.broadcast_to(counts[:, r : r + 1], (1, LANES))
    normed, inverse = norm_stats(x_ref[...].reshape(count, width).astype(F32))
    normed_b = normed.astype(BF16)
    pl.semaphore_wait(barrier, 4 + half_n - 1)

    def remote(src, dst, send, recv, peer):
        return pltpu.make_async_remote_copy(
            src_ref=src, dst_ref=dst, send_sem=send, recv_sem=recv,
            device_id=peer, device_id_type=MESH,
        )

    def gather(src, buf, base):
        near = remote(src, buf.at[1], sem_s.at[base], sem_r.at[base], core_peer)
        across = remote(src, buf.at[2], sem_s.at[base + 1], sem_r.at[base + 1], x_peer)
        onward = remote(buf.at[2], buf.at[3], sem_s.at[base + 2], sem_r.at[base + 2], core_peer)
        across.start()
        near.start()
        return near, across, onward

    c_near, c_across, c_onward = gather(cg.at[0], cg, 9)
    x_near = remote(x_ref, xg.at[1], sem_s.at[0], sem_r.at[0], core_peer)
    x_across, x_onward = [], []
    for r in range(rows):
        at = 30 + 2 * r
        x_across.append(
            remote(x_ref.at[r], xg.at[2, r], sem_s.at[at], sem_r.at[at], x_peer)
        )
        x_onward.append(
            remote(xg.at[2, r], xg.at[3, r], sem_s.at[at + 1], sem_r.at[at + 1], core_peer)
        )
        x_across[r].start()
        if r == 0:
            x_near.start()

    lane = lax.broadcasted_iota(jnp.int32, (1, QUAD), 1) // HEAD_DIM
    lane_f = [jnp.where(lane == h, 1.0, 0.0).astype(F32) for h in range(4)]
    lane_b = [m.astype(BF16) for m in lane_f]
    blocks = jnp.where(
        lax.broadcasted_iota(jnp.int32, (QUAD, QUAD), 0) // HEAD_DIM
        == lax.broadcasted_iota(jnp.int32, (QUAD, QUAD), 1) // HEAD_DIM,
        1.0 / HEAD_DIM,
        0.0,
    ).astype(BF16)
    heads = width // HEAD_DIM
    head_row = lax.broadcasted_iota(jnp.int32, (heads, width), 0)
    head_col = lax.broadcasted_iota(jnp.int32, (heads, width), 1)
    pick_sum = jnp.where(head_col // HEAD_DIM == head_row, 1.0, 0.0).astype(BF16)
    pick_one = jnp.where(head_col == head_row * HEAD_DIM, 1.0, 0.0).astype(BF16)
    place = lax.broadcasted_iota(jnp.int32, (length, LANES), 0)

    def stack(tile):
        return jnp.concatenate([tile * lane_b[h] for h in range(4)], axis=0)

    def combine(tile):
        total = tile[:HEAD_DIM] * lane_f[0]
        for h in range(1, 4):
            total = total + tile[h * length : (h + 1) * length] * lane_f[h]
        return total

    def per_row(values):
        return values.reshape(rows, length, values.shape[-1])

    def unit(raw):
        parts = []
        for start in range(0, width, QUAD):
            piece = raw[:, start : start + QUAD]
            parts.append(nn((piece * piece).astype(BF16), blocks))
        return lax.rsqrt(jnp.concatenate(parts, axis=1) + 1e-06)

    def query_of(normed_b):
        query_raw = nn(normed_b, wqkv[:, :width])
        q_inv = unit(query_raw)
        return (query_raw * q_inv).astype(BF16), query_raw, q_inv

    def mask_of(slot, r):
        return jnp.where(place < cg[slot, r : r + 1, :], 1.0, 0.0)

    def kv_of(normed_b, mask):
        mask_wide = jnp.concatenate([mask] * (width // LANES), axis=1)
        key_raw = nn(normed_b, wqkv[:, width : 2 * width])
        value = nn(normed_b, wqkv[:, 2 * width :])
        k_inv = unit(key_raw)
        key = (key_raw * k_inv * mask_wide).astype(BF16)
        return key, (value * mask_wide).astype(BF16), key_raw, k_inv, mask_wide

    mask = jnp.concatenate([mask_of(0, r) for r in range(rows)], axis=0)
    loads[0].wait()
    key, value, key_raw, k_inv, mask_wide = kv_of(normed_b, mask)
    ka[:, 0:length, :], va[:, 0:length, :] = per_row(key), per_row(value)
    ma[:, 0:length, :] = per_row(mask.astype(BF16))
    query, query_raw, q_inv = query_of(normed_b)
    qa[:, 0:length, :] = per_row(query)
    ntr[0] = normed_b.T

    c_across.wait_recv()
    c_onward.start()
    c_near.wait_recv()
    x_near.wait_recv()
    normed_near = norm_stats(xg[1].reshape(count, width).astype(F32))[0].astype(BF16)
    mask = jnp.concatenate([mask_of(1, r) for r in range(rows)], axis=0)
    key, value = kv_of(normed_near, mask)[:2]
    at = slice(length, 2 * length)
    ka[:, at, :], va[:, at, :] = per_row(key), per_row(value)
    ma[:, at, :] = per_row(mask.astype(BF16))

    logit = 8.0 / HEAD_DIM
    normed_far = []
    x_across[0].wait_recv()
    x_onward[0].start()
    c_onward.wait_recv()
    for r in range(rows):
        x_onward[r].wait_recv()
        if r + 1 < rows:
            x_across[r + 1].wait_recv()
            x_onward[r + 1].start()
        block = jnp.concatenate([xg[2, r], xg[3, r]], axis=0).astype(F32)
        normed_far.append(norm_stats(block)[0].astype(BF16))
        mask = jnp.concatenate([mask_of(2, r), mask_of(3, r)], axis=0)
        far_key, far_value = kv_of(normed_far[r], mask)[:2]
        at = slice(2 * length, 4 * length)
        ka[r, at, :], va[r, at, :], ma[r, at, :] = far_key, far_value, mask.astype(BF16)
        for qd in range(quads):
            cs = slice(qd * QUAD, (qd + 1) * QUAD)
            key, value = ka[r, :, cs], va[r, :, cs]
            score = jnp.exp(nt(stack(qa[r, 0:length, cs]), key) * logit - 8.0)
            score_b = score.astype(BF16)
            part = 1.0 / nn(score_b, ma[r])
            part = jnp.concatenate([part, part], axis=1)
            probs[r, qd] = score * part
            att_ref[r, :, cs] = combine(nn(score_b, value) * part)
            ivb_ref[r, :, cs] = combine(part)

    pending = {}

    def order(c):
        return lo, x_pos, lo_peer, x_peer

    def chunk(c):
        return bufs[9 * c : 9 * c + 9]

    def begin(c, left, right):
        part, from_core = chunk(c)[:2]
        n, r, c4 = part.shape[-3:]
        full = tn(left, right)
        for l in range(SECTORS):
            piece = full[:, l * c4 : (l + 1) * c4].reshape(n, 2, r, c4).astype(BF16)
            for low in range(2):
                part[l % 2, low, l // 2] = piece[:, low]
        at = 12 + 3 * c
        copy = remote(part.at[1 - core], from_core, sem_s.at[at], sem_r.at[at], core_peer)
        copy.start()
        pending[c] = copy

    def add(*terms):
        total = terms[0].astype(F32)
        for term in terms[1:]:
            total = total + term.astype(F32)
        return total.astype(BF16)

    def second(c):
        part, from_core, to_one, from_one = chunk(c)[:4]
        first_pos, _, first_peer, _ = order(c)
        pending[c].wait()
        to_one[...] = add(part[core, 1 - first_pos], from_core[1 - first_pos])
        at = 12 + 3 * c + 1
        copy = remote(to_one, from_one, sem_s.at[at], sem_r.at[at], first_peer)
        copy.start()
        pending[c] = copy

    def third(c):
        part, from_core, _, from_one, to_two, from_two = chunk(c)[:6]
        one, two, _, peer = order(c)
        pending[c].wait()
        to_two[...] = add(part[core, one, 1 - two], from_core[one, 1 - two], from_one[1 - two])
        at = 12 + 3 * c + 2
        copy = remote(to_two, from_two, sem_s.at[at], sem_r.at[at], peer)
        copy.start()
        pending[c] = copy

    def lat_copy(c, offset):
        total, from_lat = chunk(c)[6:8]
        target = hi_peer(offset)
        return remote(
            total.at[target], from_lat.at[offset - 1],
            lat_s.at[c, offset - 1], lat_r.at[c, offset - 1], (target * 2 + lo, lon),
        )

    def lon_send(c, grad):
        send, received = chunk(c)[:2]
        c4 = send.shape[-1]
        for l in range(SECTORS):
            send[l] = grad[:, l * c4 : (l + 1) * c4]
        copies = []
        for slot, peer in ((3, far_peer), (2, x_peer), (1, core_peer)):
            at = 12 + 3 * c + slot - 1
            copy = remote(
                send.at[peer[1]], received.at[slot - 1], sem_s.at[at], sem_r.at[at], peer
            )
            copy.start()
            copies.append(copy)
        pending[c] = copies

    def lon_sum(c):
        send, received, part, from_one = chunk(c)[:4]
        _, n, r, c4 = part.shape
        for copy in pending[c]:
            copy.wait()
        full = nn(ntr[0], send[lon])
        for slot in range(1, SECTORS):
            full = full + nn(ntr[slot], received[slot - 1])
        piece = full.reshape(n, 2, r, c4).astype(BF16)
        for low in range(2):
            part[low] = piece[:, low]
        at = 30 + 2 * rows + c - 3
        copy = remote(part.at[1 - lo], from_one, sem_s.at[at], sem_r.at[at], lo_peer)
        copy.start()
        pending[c] = copy

    def fourth(c):
        part, from_core, _, from_one, _, from_two, total, _, _ = chunk(c)
        one, two, _, _ = order(c)
        pending[c].wait()
        if c >= 3:
            total[...] = add(chunk(c)[2][lo], from_one[...])
        else:
            total[...] = add(
                part[core, one, two], from_core[one, two], from_one[two], from_two[...]
            )

        @pl.loop(1, half_n)
        def _(offset):
            lat_copy(c, offset).start()

    def fifth(c):
        total, from_lat, everyone = chunk(c)[6:9]

        @pl.loop(1, half_n)
        def _(offset):
            lat_copy(c, offset).wait()

        everyone[lon] = (
            total[hi].astype(F32) + jnp.sum(from_lat[...].astype(F32), axis=0)
        ).astype(BF16)
        copies = []
        for i, peer in enumerate((x_peer, far_peer, core_peer)):
            copy = remote(
                everyone.at[lon], everyone.at[lon], all_s.at[c, i], all_r.at[c, i], peer
            )
            copy.start()
            copies.append(copy)
        pending[c] = copies

    stores = []

    def store(src, dst):
        copy = pltpu.make_async_copy(src, dst, out_sem.at[len(stores)])
        copy.start()
        stores.append(copy)

    def finish(c, out, first):
        everyone = chunk(c)[8]
        c4 = everyone.shape[-1]
        for copy in pending[c]:
            copy.wait()
        for l in range(SECTORS):
            out[:, first + l * c4 : first + (l + 1) * c4] = everyone[l].astype(F32) * scale

    for load in loads[1:]:
        load.wait()
    tokens = x_ref[...].reshape(count, width).astype(F32)
    cotangent = cot_ref[...].reshape(count, width).astype(F32)
    grad_branch = (mask_wide * cotangent).astype(BF16)
    attended = att_ref[...].reshape(count, width)
    attended_b = attended.astype(BF16)
    middle = tokens + mask_wide * nn(attended_b, wout[...])
    normed_two, inverse_two = norm_stats(middle)
    normed_two_b = normed_two.astype(BF16)
    lifted = nn(normed_two_b, wup[...])
    root = math.sqrt(2.0 / math.pi)
    square = lifted * lifted
    curve = jnp.tanh(root * lifted * (1.0 + 0.044715 * square))
    half = 0.5 * (1.0 + curve)
    active = (lifted * half).astype(BF16)
    slope = half + 0.5 * lifted * (1.0 - curve * curve) * (root * (1.0 + 3 * 0.044715 * square))
    begin(0, active, grad_branch)

    grad_lifted = (slope * nt(grad_branch, wdown[...])).astype(BF16)
    grad_middle = cotangent + norm_back(nt(grad_lifted, wup[...]), normed_two, inverse_two)
    second(0)
    grad_attn = (mask_wide * grad_middle).astype(BF16)
    grad_attended = nt(grad_attn, wout[...]).astype(BF16)
    gaall[0] = per_row(grad_attended)
    g_near, g_across, g_onward = gather(gaall.at[0], gaall, 3)
    product = per_row(grad_attended.astype(F32) * attended)
    for r in range(rows):
        high, low = split_two(ivb_ref[r])
        part = nt(pick_one, high) + nt(pick_one, low)
        high, low = split_two(product[r])
        delta = nt(pick_sum, high) + nt(pick_sum, low)
        pair = jnp.concatenate([part, delta], axis=0)
        stats[0, r] = jnp.concatenate([pair, jnp.zeros_like(pair)], axis=1)
    s_near, s_across, s_onward = gather(stats.at[0], stats, 6)

    begin(1, normed_two_b, grad_lifted)
    begin(2, attended_b, grad_attn)
    second(1)
    second(2)
    qa[:, length : 2 * length, :] = per_row(query_of(normed_near)[0])
    qa[:, 2 * length : 4 * length, :] = query_of(
        jnp.concatenate(normed_far, axis=0)
    )[0].reshape(rows, 2 * length, width)
    ntr[1] = normed_near.T
    ntr[2] = jnp.concatenate([piece[:length] for piece in normed_far], axis=0).T
    ntr[3] = jnp.concatenate([piece[length:] for piece in normed_far], axis=0).T
    third(0)
    g_across.wait_recv()
    g_onward.start()
    s_across.wait_recv()
    s_onward.start()

    for r in range(rows):
        for qd in range(quads):
            cs = slice(qd * QUAD, (qd + 1) * QUAD)
            key, value = ka[r, :, cs], va[r, :, cs]
            tall = stack(gaall[0, r, :, cs])
            delta = jnp.sum(
                tall.astype(F32) * jnp.concatenate([att_ref[r, :, cs]] * 4, axis=0),
                axis=-1,
                keepdims=True,
            )
            back = (probs[r, qd] * (nt(tall, value) - delta) * logit).astype(BF16)
            dq_ref[r, :, cs] = combine(nn(back, key))

    def head_back(grad, raw, inv):
        return inv * (grad - raw * (inv * inv) * head_mean(raw * grad, blocks))

    grad_q = head_back(dq_ref[...].reshape(count, width), query_raw, q_inv).astype(BF16)
    lon_send(3, grad_q)
    for copy in (g_near, s_near, g_onward, s_onward):
        copy.wait_recv()
    third(1)

    for r in range(rows):
        stat = jnp.concatenate([stats[s, r][:, :length] for s in range(SECTORS)], axis=1)
        for qd in range(quads):
            cs = slice(qd * QUAD, (qd + 1) * QUAD)
            query = qa[r, :, cs]
            grad = jnp.concatenate([gaall[s, r, :, cs] for s in range(SECTORS)], axis=0)

            def spread(base):
                return jnp.concatenate(
                    [
                        jnp.broadcast_to(stat[base + h : base + h + 1], (length, QUAD))
                        for h in range(qd * 4, qd * 4 + 4)
                    ],
                    axis=0,
                )

            score = jnp.exp(nt(stack(ka[r, 0:length, cs]), query) * logit - 8.0) * spread(0)
            deep = nt(stack(va[r, 0:length, cs]), grad)
            back = (score * (deep - spread(heads)) * logit).astype(BF16)
            dk_ref[r, :, cs] = combine(nn(back, query))
            dv_ref[r, :, cs] = combine(nn(score.astype(BF16), grad))

    grad_v = (dv_ref[...].reshape(count, width) * mask_wide).astype(BF16)
    lon_send(4, grad_v)
    third(2)
    fourth(0)
    grad_k = head_back(
        dk_ref[...].reshape(count, width) * mask_wide, key_raw, k_inv
    ).astype(BF16)
    lon_send(5, grad_k)
    lon_sum(3)
    fourth(1)
    fourth(2)
    fifth(0)
    lon_sum(4)
    grad_normed = (
        nt(grad_q, wqkv[:, :width])
        + nt(grad_k, wqkv[:, width : 2 * width])
        + nt(grad_v, wqkv[:, 2 * width :])
    )
    gt_ref[...] = per_row((grad_middle + norm_back(grad_normed, normed, inverse)).astype(BF16))
    store(gt_ref, gt_hbm)
    lon_sum(5)
    fourth(3)
    bo_ref[...] = per_row((middle + mask_wide * nn(active, wdown[...])).astype(BF16))
    store(bo_ref, bo_hbm)
    fourth(4)
    fifth(1)
    fourth(5)
    finish(0, gdown, 0)
    store(gdown, gdown_hbm)
    fifth(2)
    fifth(3)
    finish(1, gup, 0)
    store(gup, gup_hbm)
    fifth(4)
    finish(2, gout, 0)
    store(gout, gout_hbm)
    finish(3, gqkv, 0)
    for group in (
        (g_near, g_across, g_onward), (s_near, s_across, s_onward),
        [x_near] + x_across + x_onward, (c_near, c_across, c_onward),
    ):
        for copy in group:
            copy.wait_send()
    fifth(5)
    finish(4, gqkv, 2 * width)
    finish(5, gqkv, width)
    store(gqkv, gqkv_hbm)
    for copy in stores:
        copy.wait()


def hand_over(*refs):
    sems = refs[12]
    copies = [pltpu.make_async_copy(refs[i], refs[6 + i], sems.at[i]) for i in range(6)]
    for copy in copies:
        copy.start()
    for copy in copies:
        copy.wait()


def local(lat_n, tokens, ocean_count, w_qkv, w_out, w_up, w_down, cotangent):
    rows, length, width = tokens.shape
    heads = width // HEAD_DIM
    hidden = w_up.shape[1]
    half_n = lat_n // 2
    scale = 1.0 / math.sqrt(rows * lat_n * length * SECTORS)
    quads = width // QUAD
    full = length * SECTORS
    out_shape = (
        jax.ShapeDtypeStruct(tokens.shape, BF16),
        jax.ShapeDtypeStruct(tokens.shape, BF16),
        jax.ShapeDtypeStruct((width // lat_n, 3 * width), F32),
        jax.ShapeDtypeStruct((width // lat_n, width), F32),
        jax.ShapeDtypeStruct((width // lat_n, hidden), F32),
        jax.ShapeDtypeStruct((hidden // lat_n, width), F32),
    )
    scratch = [pltpu.VMEM(a.shape, BF16) for a in (cotangent, w_qkv, w_out, w_up, w_down)]
    scratch += [pltpu.VMEM(a.shape, a.dtype) for a in out_shape]
    scratch += [
        pltpu.VMEM((SECTORS, rows, length, width), BF16),
        pltpu.VMEM((SECTORS, -(-rows // 8) * 8, LANES), jnp.int32),
        pltpu.VMEM((rows, full, width), BF16),
        pltpu.VMEM((rows, full, width), BF16),
        pltpu.VMEM((rows, full, LANES), BF16),
        pltpu.VMEM((rows, full, width), BF16),
        pltpu.VMEM((rows, quads, 4 * length, full), F32),
        pltpu.VMEM((rows, length, width), F32),
        pltpu.VMEM((rows, length, width), F32),
        pltpu.VMEM((rows, length, width), F32),
        pltpu.VMEM((rows, length, width), F32),
        pltpu.VMEM((rows, length, width), F32),
        pltpu.VMEM((SECTORS, rows, length, width), BF16),
        pltpu.VMEM((SECTORS, rows, 2 * heads, LANES), F32),
        pltpu.VMEM((SECTORS, width, rows * length), BF16),
        pltpu.SemaphoreType.DMA((33 + 2 * rows,)),
        pltpu.SemaphoreType.DMA((33 + 2 * rows,)),
        pltpu.SemaphoreType.DMA((6, half_n - 1)),
        pltpu.SemaphoreType.DMA((6, half_n - 1)),
        pltpu.SemaphoreType.DMA((6, 3)),
        pltpu.SemaphoreType.DMA((6, 3)),
        pltpu.SemaphoreType.DMA((5,)),
        pltpu.SemaphoreType.DMA((6,)),
    ]
    for c, (tall, broad) in enumerate(
        ((hidden, width), (width, hidden)) + ((width, width),) * 4
    ):
        r, c4 = tall // lat_n, broad // SECTORS
        if c < 3:
            scratch += [
                pltpu.VMEM((2, 2, 2, half_n, r, c4), BF16),
                pltpu.VMEM((2, 2, half_n, r, c4), BF16),
                pltpu.VMEM((2, half_n, r, c4), BF16),
                pltpu.VMEM((2, half_n, r, c4), BF16),
                pltpu.VMEM((half_n, r, c4), BF16),
                pltpu.VMEM((half_n, r, c4), BF16),
            ]
        else:
            scratch += [
                pltpu.VMEM((SECTORS, rows * length, c4), BF16),
                pltpu.VMEM((SECTORS - 1, rows * length, c4), BF16),
                pltpu.VMEM((2, half_n, r, c4), BF16),
                pltpu.VMEM((half_n, r, c4), BF16),
                pltpu.VMEM((8, LANES), BF16),
                pltpu.VMEM((8, LANES), BF16),
            ]
        scratch += [
            pltpu.VMEM((half_n, r, c4), BF16),
            pltpu.VMEM((half_n - 1, r, c4), BF16),
            pltpu.VMEM((SECTORS, r, c4), BF16),
        ]
    vmem = pl.BlockSpec(memory_space=pltpu.VMEM)
    hbm = pl.BlockSpec(memory_space=pl.ANY)
    results = pl.pallas_call(
        functools.partial(kernel, lat_n, scale),
        out_shape=out_shape,
        in_specs=[vmem] * 2 + [hbm] * 5,
        out_specs=(hbm,) * 6,
        scratch_shapes=scratch,
        compiler_params=pltpu.CompilerParams(
            collective_id=0, has_side_effects=True, vmem_limit_bytes=56 * 1024 * 1024
        ),
    )(tokens, ocean_count.T, cotangent, w_qkv, w_out, w_up, w_down)
    return pl.pallas_call(
        hand_over,
        out_shape=out_shape,
        in_specs=[vmem] * 6,
        out_specs=(hbm,) * 6,
        scratch_shapes=[pltpu.SemaphoreType.DMA((6,))],
    )(*results)


def solution(mesh):
    rows = P("lat", "lon", None)
    in_specs = (rows, P("lat", "lon"), P(), P(), P(), P(), rows)
    out_specs = (rows, rows, P("lat", None), P("lat", None), P("lat", None), P("lat", None))
    return jax.shard_map(
        functools.partial(local, mesh.shape["lat"]),
        mesh=mesh,
        in_specs=in_specs,
        out_specs=out_specs,
        check_vma=False,
    )
```

```python
import functools
import math

import jax
import jax.numpy as jnp
from jax import lax
from jax.experimental import pallas as pl
from jax.experimental.pallas import tpu as pltpu
from jax.sharding import PartitionSpec as P

HEAD_DIM = 64
SECTORS = 4
QUAD = 4 * HEAD_DIM
LANES = 128
MESH = pl.DeviceIdType.MESH
F32 = jnp.float32
BF16 = jnp.bfloat16


def nn(a, b):
    return jnp.dot(a, b, preferred_element_type=F32)


def nt(a, b):
    return lax.dot_general(a, b, (((1,), (1,)), ((), ())), preferred_element_type=F32)


def tn(a, b):
    return lax.dot_general(a, b, (((0,), (0,)), ((), ())), preferred_element_type=F32)


def split_two(values):
    high = values.astype(BF16)
    return high, (values - high.astype(F32)).astype(BF16)


def norm_stats(values):
    average = jnp.mean(values, axis=-1, keepdims=True)
    centered = values - average
    variance = jnp.mean(centered * centered, axis=-1, keepdims=True)
    inverse = lax.rsqrt(variance + 1e-05)
    return centered * inverse, inverse


def norm_back(grad, normed, inverse):
    first = jnp.mean(grad, axis=-1, keepdims=True)
    second = jnp.mean(grad * normed, axis=-1, keepdims=True)
    return inverse * (grad - first - normed * second)


def head_mean(values, blocks):
    parts = []
    for start in range(0, values.shape[1], QUAD):
        parts.append(nn(values[:, start : start + QUAD].astype(BF16), blocks))
    return jnp.concatenate(parts, axis=1)


def kernel(lat_n, scale, *refs):
    x_ref, count_ref, cot_hbm, wqkv_hbm, wout_hbm, wup_hbm, wdown_hbm = refs[:7]
    bo_hbm, gt_hbm, gqkv_hbm, gout_hbm, gup_hbm, gdown_hbm = refs[7:13]
    cot_ref, wqkv, wout, wup, wdown = refs[13:18]
    bo_ref, gt_ref, gqkv, gout, gup, gdown = refs[18:24]
    xg, cg, ka, va, ma, qa, probs, att_ref, ivb_ref, dq_ref, dk_ref, dv_ref, gaall, stats, ntr = refs[24:39]
    sem_s, sem_r, lat_s, lat_r, all_s, all_r, in_sem, out_sem = refs[39:47]
    bufs = refs[47:]
    rows, length, width = x_ref.shape
    count = rows * length
    quads = width // QUAD
    half_n = lat_n // 2

    lat = lax.axis_index("lat")
    lon = lax.axis_index("lon")
    x_pos, core = lon // 2, lon % 2
    hi, lo = lat // 2, lat % 2
    core_peer = (lat, x_pos * 2 + (1 - core))
    x_peer = (lat, (1 - x_pos) * 2 + core)
    far_peer = (lat, (1 - x_pos) * 2 + (1 - core))
    lo_peer = (hi * 2 + (1 - lo), lon)

    barrier = pltpu.get_barrier_semaphore()
    for peer in (core_peer, x_peer, far_peer, lo_peer):
        pl.semaphore_signal(barrier, inc=1, device_id=peer, device_id_type=MESH)

    def hi_peer(offset):
        return lax.rem(hi + offset, half_n)

    @pl.loop(1, half_n)
    def _(offset):
        pl.semaphore_signal(
            barrier, inc=1, device_id=(hi_peer(offset) * 2 + lo, lon), device_id_type=MESH
        )

    loads = []
    for i, (src, dst) in enumerate(
        ((wqkv_hbm, wqkv), (wout_hbm, wout), (cot_hbm, cot_ref), (wup_hbm, wup), (wdown_hbm, wdown))
    ):
        load = pltpu.make_async_copy(src, dst, in_sem.at[i])
        load.start()
        loads.append(load)

    cg[0] = jnp.zeros_like(cg[0])
    counts = count_ref[...]
    for r in range(rows):
        cg[0, r : r + 1] = jnp.broadcast_to(counts[:, r : r + 1], (1, LANES))
    normed, inverse = norm_stats(x_ref[...].reshape(count, width).astype(F32))
    normed_b = normed.astype(BF16)
    pl.semaphore_wait(barrier, 4 + half_n - 1)

    def remote(src, dst, send, recv, peer):
        return pltpu.make_async_remote_copy(
            src_ref=src, dst_ref=dst, send_sem=send, recv_sem=recv,
            device_id=peer, device_id_type=MESH,
        )

    def gather(src, buf, base):
        near = remote(src, buf.at[1], sem_s.at[base], sem_r.at[base], core_peer)
        across = remote(src, buf.at[2], sem_s.at[base + 1], sem_r.at[base + 1], x_peer)
        onward = remote(buf.at[2], buf.at[3], sem_s.at[base + 2], sem_r.at[base + 2], core_peer)
        across.start()
        near.start()
        return near, across, onward

    c_near, c_across, c_onward = gather(cg.at[0], cg, 9)
    x_near = remote(x_ref, xg.at[1], sem_s.at[0], sem_r.at[0], core_peer)
    x_across, x_onward = [], []
    for r in range(rows):
        at = 30 + 2 * r
        x_across.append(
            remote(x_ref.at[r], xg.at[2, r], sem_s.at[at], sem_r.at[at], x_peer)
        )
        x_onward.append(
            remote(xg.at[2, r], xg.at[3, r], sem_s.at[at + 1], sem_r.at[at + 1], core_peer)
        )
        x_across[r].start()
        if r == 0:
            x_near.start()

    lane = lax.broadcasted_iota(jnp.int32, (1, QUAD), 1) // HEAD_DIM
    lane_f = [jnp.where(lane == h, 1.0, 0.0).astype(F32) for h in range(4)]
    lane_b = [m.astype(BF16) for m in lane_f]
    blocks = jnp.where(
        lax.broadcasted_iota(jnp.int32, (QUAD, QUAD), 0) // HEAD_DIM
        == lax.broadcasted_iota(jnp.int32, (QUAD, QUAD), 1) // HEAD_DIM,
        1.0 / HEAD_DIM,
        0.0,
    ).astype(BF16)
    heads = width // HEAD_DIM
    head_row = lax.broadcasted_iota(jnp.int32, (heads, width), 0)
    head_col = lax.broadcasted_iota(jnp.int32, (heads, width), 1)
    pick_sum = jnp.where(head_col // HEAD_DIM == head_row, 1.0, 0.0).astype(BF16)
    pick_one = jnp.where(head_col == head_row * HEAD_DIM, 1.0, 0.0).astype(BF16)
    place = lax.broadcasted_iota(jnp.int32, (length, LANES), 0)

    def stack(tile):
        return jnp.concatenate([tile * lane_b[h] for h in range(4)], axis=0)

    def combine(tile):
        total = tile[:HEAD_DIM] * lane_f[0]
        for h in range(1, 4):
            total = total + tile[h * length : (h + 1) * length] * lane_f[h]
        return total

    def per_row(values):
        return values.reshape(rows, length, values.shape[-1])

    def unit(raw):
        parts = []
        for start in range(0, width, QUAD):
            piece = raw[:, start : start + QUAD]
            parts.append(nn((piece * piece).astype(BF16), blocks))
        return lax.rsqrt(jnp.concatenate(parts, axis=1) + 1e-06)

    def query_of(normed_b):
        query_raw = nn(normed_b, wqkv[:, :width])
        q_inv = unit(query_raw)
        return (query_raw * q_inv).astype(BF16), query_raw, q_inv

    def mask_of(slot, r):
        return jnp.where(place < cg[slot, r : r + 1, :], 1.0, 0.0)

    def kv_of(normed_b, mask):
        mask_wide = jnp.concatenate([mask] * (width // LANES), axis=1)
        key_raw = nn(normed_b, wqkv[:, width : 2 * width])
        value = nn(normed_b, wqkv[:, 2 * width :])
        k_inv = unit(key_raw)
        key = (key_raw * k_inv * mask_wide).astype(BF16)
        return key, (value * mask_wide).astype(BF16), key_raw, k_inv, mask_wide

    mask = jnp.concatenate([mask_of(0, r) for r in range(rows)], axis=0)
    loads[0].wait()
    key, value, key_raw, k_inv, mask_wide = kv_of(normed_b, mask)
    ka[:, 0:length, :], va[:, 0:length, :] = per_row(key), per_row(value)
    ma[:, 0:length, :] = per_row(mask.astype(BF16))
    query, query_raw, q_inv = query_of(normed_b)
    qa[:, 0:length, :] = per_row(query)
    ntr[0] = normed_b.T

    c_across.wait_recv()
    c_onward.start()
    c_near.wait_recv()
    x_near.wait_recv()
    normed_near = norm_stats(xg[1].reshape(count, width).astype(F32))[0].astype(BF16)
    mask = jnp.concatenate([mask_of(1, r) for r in range(rows)], axis=0)
    key, value = kv_of(normed_near, mask)[:2]
    at = slice(length, 2 * length)
    ka[:, at, :], va[:, at, :] = per_row(key), per_row(value)
    ma[:, at, :] = per_row(mask.astype(BF16))

    logit = 8.0 / HEAD_DIM
    normed_far = []
    x_across[0].wait_recv()
    x_onward[0].start()
    c_onward.wait_recv()
    for r in range(rows):
        x_onward[r].wait_recv()
        if r + 1 < rows:
            x_across[r + 1].wait_recv()
            x_onward[r + 1].start()
        block = jnp.concatenate([xg[2, r], xg[3, r]], axis=0).astype(F32)
        normed_far.append(norm_stats(block)[0].astype(BF16))
        mask = jnp.concatenate([mask_of(2, r), mask_of(3, r)], axis=0)
        far_key, far_value = kv_of(normed_far[r], mask)[:2]
        at = slice(2 * length, 4 * length)
        ka[r, at, :], va[r, at, :], ma[r, at, :] = far_key, far_value, mask.astype(BF16)
        for qd in range(quads):
            cs = slice(qd * QUAD, (qd + 1) * QUAD)
            key, value = ka[r, :, cs], va[r, :, cs]
            score = jnp.exp(nt(stack(qa[r, 0:length, cs]), key) * logit - 8.0)
            score_b = score.astype(BF16)
            part = 1.0 / nn(score_b, ma[r])
            part = jnp.concatenate([part, part], axis=1)
            probs[r, qd] = score * part
            att_ref[r, :, cs] = combine(nn(score_b, value) * part)
            ivb_ref[r, :, cs] = combine(part)

    pending = {}

    def order(c):
        return lo, x_pos, lo_peer, x_peer

    def chunk(c):
        return bufs[9 * c : 9 * c + 9]

    def begin(c, left, right):
        part, from_core = chunk(c)[:2]
        n, r, c4 = part.shape[-3:]
        full = tn(left, right)
        for l in range(SECTORS):
            piece = full[:, l * c4 : (l + 1) * c4].reshape(n, 2, r, c4).astype(BF16)
            for low in range(2):
                part[l % 2, low, l // 2] = piece[:, low]
        at = 12 + 3 * c
        copy = remote(part.at[1 - core], from_core, sem_s.at[at], sem_r.at[at], core_peer)
        copy.start()
        pending[c] = copy

    def add(*terms):
        total = terms[0].astype(F32)
        for term in terms[1:]:
            total = total + term.astype(F32)
        return total.astype(BF16)

    def second(c):
        part, from_core, to_one, from_one = chunk(c)[:4]
        first_pos, _, first_peer, _ = order(c)
        pending[c].wait()
        to_one[...] = add(part[core, 1 - first_pos], from_core[1 - first_pos])
        at = 12 + 3 * c + 1
        copy = remote(to_one, from_one, sem_s.at[at], sem_r.at[at], first_peer)
        copy.start()
        pending[c] = copy

    def third(c):
        part, from_core, _, from_one, to_two, from_two = chunk(c)[:6]
        one, two, _, peer = order(c)
        pending[c].wait()
        to_two[...] = add(part[core, one, 1 - two], from_core[one, 1 - two], from_one[1 - two])
        at = 12 + 3 * c + 2
        copy = remote(to_two, from_two, sem_s.at[at], sem_r.at[at], peer)
        copy.start()
        pending[c] = copy

    def lat_copy(c, offset):
        total, from_lat = chunk(c)[6:8]
        target = hi_peer(offset)
        return remote(
            total.at[target], from_lat.at[offset - 1],
            lat_s.at[c, offset - 1], lat_r.at[c, offset - 1], (target * 2 + lo, lon),
        )

    def lon_send(c, grad):
        send, received = chunk(c)[:2]
        c4 = send.shape[-1]
        for l in range(SECTORS):
            send[l] = grad[:, l * c4 : (l + 1) * c4]
        copies = []
        for slot, peer in ((3, far_peer), (2, x_peer), (1, core_peer)):
            at = 12 + 3 * c + slot - 1
            copy = remote(
                send.at[peer[1]], received.at[slot - 1], sem_s.at[at], sem_r.at[at], peer
            )
            copy.start()
            copies.append(copy)
        pending[c] = copies

    def lon_sum(c):
        send, received, part, from_one = chunk(c)[:4]
        _, n, r, c4 = part.shape
        for copy in pending[c]:
            copy.wait()
        full = nn(ntr[0], send[lon])
        for slot in range(1, SECTORS):
            full = full + nn(ntr[slot], received[slot - 1])
        piece = full.reshape(n, 2, r, c4).astype(BF16)
        for low in range(2):
            part[low] = piece[:, low]
        at = 30 + 2 * rows + c - 3
        copy = remote(part.at[1 - lo], from_one, sem_s.at[at], sem_r.at[at], lo_peer)
        copy.start()
        pending[c] = copy

    def fourth(c):
        part, from_core, _, from_one, _, from_two, total, _, _ = chunk(c)
        one, two, _, _ = order(c)
        pending[c].wait()
        if c >= 3:
            total[...] = add(chunk(c)[2][lo], from_one[...])
        else:
            total[...] = add(
                part[core, one, two], from_core[one, two], from_one[two], from_two[...]
            )

        @pl.loop(1, half_n)
        def _(offset):
            lat_copy(c, offset).start()

    def fifth(c):
        total, from_lat, everyone = chunk(c)[6:9]

        @pl.loop(1, half_n)
        def _(offset):
            lat_copy(c, offset).wait()

        everyone[lon] = (
            total[hi].astype(F32) + jnp.sum(from_lat[...].astype(F32), axis=0)
        ).astype(BF16)
        copies = []
        for i, peer in enumerate((x_peer, far_peer, core_peer)):
            copy = remote(
                everyone.at[lon], everyone.at[lon], all_s.at[c, i], all_r.at[c, i], peer
            )
            copy.start()
            copies.append(copy)
        pending[c] = copies

    stores = []

    def store(src, dst):
        copy = pltpu.make_async_copy(src, dst, out_sem.at[len(stores)])
        copy.start()
        stores.append(copy)

    def finish(c, out, first):
        everyone = chunk(c)[8]
        c4 = everyone.shape[-1]
        for copy in pending[c]:
            copy.wait()
        for l in range(SECTORS):
            out[:, first + l * c4 : first + (l + 1) * c4] = everyone[l].astype(F32) * scale

    for load in loads[1:]:
        load.wait()
    tokens = x_ref[...].reshape(count, width).astype(F32)
    cotangent = cot_ref[...].reshape(count, width).astype(F32)
    grad_branch = (mask_wide * cotangent).astype(BF16)
    attended = att_ref[...].reshape(count, width)
    attended_b = attended.astype(BF16)
    middle = tokens + mask_wide * nn(attended_b, wout[...])
    normed_two, inverse_two = norm_stats(middle)
    normed_two_b = normed_two.astype(BF16)
    lifted = nn(normed_two_b, wup[...])
    root = math.sqrt(2.0 / math.pi)
    square = lifted * lifted
    curve = jnp.tanh(root * lifted * (1.0 + 0.044715 * square))
    half = 0.5 * (1.0 + curve)
    active = (lifted * half).astype(BF16)
    slope = half + 0.5 * lifted * (1.0 - curve * curve) * (root * (1.0 + 3 * 0.044715 * square))
    begin(0, active, grad_branch)

    grad_lifted = (slope * nt(grad_branch, wdown[...])).astype(BF16)
    grad_middle = cotangent + norm_back(nt(grad_lifted, wup[...]), normed_two, inverse_two)
    second(0)
    grad_attn = (mask_wide * grad_middle).astype(BF16)
    grad_attended = nt(grad_attn, wout[...]).astype(BF16)
    gaall[0] = per_row(grad_attended)
    g_near, g_across, g_onward = gather(gaall.at[0], gaall, 3)
    product = per_row(grad_attended.astype(F32) * attended)
    for r in range(rows):
        high, low = split_two(ivb_ref[r])
        part = nt(pick_one, high) + nt(pick_one, low)
        high, low = split_two(product[r])
        delta = nt(pick_sum, high) + nt(pick_sum, low)
        pair = jnp.concatenate([part, delta], axis=0)
        stats[0, r] = jnp.concatenate([pair, jnp.zeros_like(pair)], axis=1)
    s_near, s_across, s_onward = gather(stats.at[0], stats, 6)

    begin(1, normed_two_b, grad_lifted)
    begin(2, attended_b, grad_attn)
    second(1)
    second(2)
    qa[:, length : 2 * length, :] = per_row(query_of(normed_near)[0])
    qa[:, 2 * length : 4 * length, :] = query_of(
        jnp.concatenate(normed_far, axis=0)
    )[0].reshape(rows, 2 * length, width)
    g_across.wait_recv()
    g_onward.start()
    s_across.wait_recv()
    s_onward.start()

    for r in range(rows):
        for qd in range(quads):
            cs = slice(qd * QUAD, (qd + 1) * QUAD)
            key, value = ka[r, :, cs], va[r, :, cs]
            tall = stack(gaall[0, r, :, cs])
            delta = jnp.sum(
                tall.astype(F32) * jnp.concatenate([att_ref[r, :, cs]] * 4, axis=0),
                axis=-1,
                keepdims=True,
            )
            back = (probs[r, qd] * (nt(tall, value) - delta) * logit).astype(BF16)
            dq_ref[r, :, cs] = combine(nn(back, key))

    def head_back(grad, raw, inv):
        return inv * (grad - raw * (inv * inv) * head_mean(raw * grad, blocks))

    grad_q = head_back(dq_ref[...].reshape(count, width), query_raw, q_inv).astype(BF16)
    lon_send(3, grad_q)
    third(0)
    for copy in (g_near, s_near, g_onward, s_onward):
        copy.wait_recv()

    for r in range(rows):
        stat = jnp.concatenate([stats[s, r][:, :length] for s in range(SECTORS)], axis=1)
        for qd in range(quads):
            cs = slice(qd * QUAD, (qd + 1) * QUAD)
            query = qa[r, :, cs]
            grad = jnp.concatenate([gaall[s, r, :, cs] for s in range(SECTORS)], axis=0)

            def spread(base):
                return jnp.concatenate(
                    [
                        jnp.broadcast_to(stat[base + h : base + h + 1], (length, QUAD))
                        for h in range(qd * 4, qd * 4 + 4)
                    ],
                    axis=0,
                )

            score = jnp.exp(nt(stack(ka[r, 0:length, cs]), query) * logit - 8.0) * spread(0)
            deep = nt(stack(va[r, 0:length, cs]), grad)
            back = (score * (deep - spread(heads)) * logit).astype(BF16)
            dk_ref[r, :, cs] = combine(nn(back, query))
            dv_ref[r, :, cs] = combine(nn(score.astype(BF16), grad))

    grad_v = (dv_ref[...].reshape(count, width) * mask_wide).astype(BF16)
    lon_send(4, grad_v)
    grad_k = head_back(
        dk_ref[...].reshape(count, width) * mask_wide, key_raw, k_inv
    ).astype(BF16)
    lon_send(5, grad_k)
    third(1)
    ntr[1] = normed_near.T
    ntr[2] = jnp.concatenate([piece[:length] for piece in normed_far], axis=0).T
    ntr[3] = jnp.concatenate([piece[length:] for piece in normed_far], axis=0).T
    lon_sum(3)
    third(2)
    fourth(0)
    lon_sum(4)
    grad_normed = (
        nt(grad_q, wqkv[:, :width])
        + nt(grad_k, wqkv[:, width : 2 * width])
        + nt(grad_v, wqkv[:, 2 * width :])
    )
    gt_ref[...] = per_row((grad_middle + norm_back(grad_normed, normed, inverse)).astype(BF16))
    store(gt_ref, gt_hbm)
    lon_sum(5)
    fourth(3)
    fourth(1)
    bo_ref[...] = per_row((middle + mask_wide * nn(active, wdown[...])).astype(BF16))
    store(bo_ref, bo_hbm)
    fourth(4)
    fifth(0)
    fourth(2)
    fourth(5)
    fifth(3)
    fifth(1)
    finish(0, gdown, 0)
    store(gdown, gdown_hbm)
    fifth(4)
    fifth(2)
    finish(1, gup, 0)
    store(gup, gup_hbm)
    finish(3, gqkv, 0)
    for group in (
        (g_near, g_across, g_onward), (s_near, s_across, s_onward),
        [x_near] + x_across + x_onward, (c_near, c_across, c_onward),
    ):
        for copy in group:
            copy.wait_send()
    fifth(5)
    finish(2, gout, 0)
    store(gout, gout_hbm)
    finish(4, gqkv, 2 * width)
    finish(5, gqkv, width)
    store(gqkv, gqkv_hbm)
    for copy in stores:
        copy.wait()


def hand_over(*refs):
    sems = refs[12]
    copies = [pltpu.make_async_copy(refs[i], refs[6 + i], sems.at[i]) for i in range(6)]
    for copy in copies:
        copy.start()
    for copy in copies:
        copy.wait()


def local(lat_n, tokens, ocean_count, w_qkv, w_out, w_up, w_down, cotangent):
    rows, length, width = tokens.shape
    heads = width // HEAD_DIM
    hidden = w_up.shape[1]
    half_n = lat_n // 2
    scale = 1.0 / math.sqrt(rows * lat_n * length * SECTORS)
    quads = width // QUAD
    full = length * SECTORS
    out_shape = (
        jax.ShapeDtypeStruct(tokens.shape, BF16),
        jax.ShapeDtypeStruct(tokens.shape, BF16),
        jax.ShapeDtypeStruct((width // lat_n, 3 * width), F32),
        jax.ShapeDtypeStruct((width // lat_n, width), F32),
        jax.ShapeDtypeStruct((width // lat_n, hidden), F32),
        jax.ShapeDtypeStruct((hidden // lat_n, width), F32),
    )
    scratch = [pltpu.VMEM(a.shape, BF16) for a in (cotangent, w_qkv, w_out, w_up, w_down)]
    scratch += [pltpu.VMEM(a.shape, a.dtype) for a in out_shape]
    scratch += [
        pltpu.VMEM((SECTORS, rows, length, width), BF16),
        pltpu.VMEM((SECTORS, -(-rows // 8) * 8, LANES), jnp.int32),
        pltpu.VMEM((rows, full, width), BF16),
        pltpu.VMEM((rows, full, width), BF16),
        pltpu.VMEM((rows, full, LANES), BF16),
        pltpu.VMEM((rows, full, width), BF16),
        pltpu.VMEM((rows, quads, 4 * length, full), F32),
        pltpu.VMEM((rows, length, width), F32),
        pltpu.VMEM((rows, length, width), F32),
        pltpu.VMEM((rows, length, width), F32),
        pltpu.VMEM((rows, length, width), F32),
        pltpu.VMEM((rows, length, width), F32),
        pltpu.VMEM((SECTORS, rows, length, width), BF16),
        pltpu.VMEM((SECTORS, rows, 2 * heads, LANES), F32),
        pltpu.VMEM((SECTORS, width, rows * length), BF16),
        pltpu.SemaphoreType.DMA((33 + 2 * rows,)),
        pltpu.SemaphoreType.DMA((33 + 2 * rows,)),
        pltpu.SemaphoreType.DMA((6, half_n - 1)),
        pltpu.SemaphoreType.DMA((6, half_n - 1)),
        pltpu.SemaphoreType.DMA((6, 3)),
        pltpu.SemaphoreType.DMA((6, 3)),
        pltpu.SemaphoreType.DMA((5,)),
        pltpu.SemaphoreType.DMA((6,)),
    ]
    for c, (tall, broad) in enumerate(
        ((hidden, width), (width, hidden)) + ((width, width),) * 4
    ):
        r, c4 = tall // lat_n, broad // SECTORS
        if c < 3:
            scratch += [
                pltpu.VMEM((2, 2, 2, half_n, r, c4), BF16),
                pltpu.VMEM((2, 2, half_n, r, c4), BF16),
                pltpu.VMEM((2, half_n, r, c4), BF16),
                pltpu.VMEM((2, half_n, r, c4), BF16),
                pltpu.VMEM((half_n, r, c4), BF16),
                pltpu.VMEM((half_n, r, c4), BF16),
            ]
        else:
            scratch += [
                pltpu.VMEM((SECTORS, rows * length, c4), BF16),
                pltpu.VMEM((SECTORS - 1, rows * length, c4), BF16),
                pltpu.VMEM((2, half_n, r, c4), BF16),
                pltpu.VMEM((half_n, r, c4), BF16),
                pltpu.VMEM((8, LANES), BF16),
                pltpu.VMEM((8, LANES), BF16),
            ]
        scratch += [
            pltpu.VMEM((half_n, r, c4), BF16),
            pltpu.VMEM((half_n - 1, r, c4), BF16),
            pltpu.VMEM((SECTORS, r, c4), BF16),
        ]
    vmem = pl.BlockSpec(memory_space=pltpu.VMEM)
    hbm = pl.BlockSpec(memory_space=pl.ANY)
    results = pl.pallas_call(
        functools.partial(kernel, lat_n, scale),
        out_shape=out_shape,
        in_specs=[vmem] * 2 + [hbm] * 5,
        out_specs=(hbm,) * 6,
        scratch_shapes=scratch,
        compiler_params=pltpu.CompilerParams(
            collective_id=0, has_side_effects=True, vmem_limit_bytes=56 * 1024 * 1024
        ),
    )(tokens, ocean_count.T, cotangent, w_qkv, w_out, w_up, w_down)
    return pl.pallas_call(
        hand_over,
        out_shape=out_shape,
        in_specs=[vmem] * 6,
        out_specs=(hbm,) * 6,
        scratch_shapes=[pltpu.SemaphoreType.DMA((6,))],
    )(*results)


def solution(mesh):
    rows = P("lat", "lon", None)
    in_specs = (rows, P("lat", "lon"), P(), P(), P(), P(), rows)
    out_specs = (rows, rows, P("lat", None), P("lat", None), P("lat", None), P("lat", None))
    return jax.shard_map(
        functools.partial(local, mesh.shape["lat"]),
        mesh=mesh,
        in_specs=in_specs,
        out_specs=out_specs,
        check_vma=False,
    )
```
